768 devices in a mesh: grp: 8 (over x, core), dev: 96 (over z, y).
Axes of the slice: x: 4, y: 8, z: 12, core: 2. Of those that a mesh axis runs over, the one named last changes fastest.
Arguments:
- query_states: bfloat16 [24576, 1024], P(('grp', 'dev')), may hold values from -6 to 6
- passage_states: bfloat16 [6144, 1024], P(('grp', 'dev')), may hold values from -6 to 6
- head_weight: bfloat16 [1024, 1024], replicated, may hold values from -0.1875 to 0.1875
- candidates: int32 [24576, 256], P(('grp', 'dev')), may hold values from 0 to 767, all different within a row
- counts: int32 [24576], P(('grp', 'dev')), may hold values from 1 to 256, 3932160 in all
- teacher_scores: float32 [24576, 256], P(('grp', 'dev')), may hold values from -304 to 304
- owner_map: int32 [8, 768], P('grp'), may hold values from 0 to 767, each once within a row
Outputs:
- query_grad: bfloat16 [24576, 1024], P(('grp', 'dev'))
- passage_grad: bfloat16 [6144, 1024], P(('grp', 'dev'))
- head_grad: float32 [1024, 1024], P('grp')
The draws below stay inside these ranges and needn't reach their ends.
Inputs may be any that keep to these rules, and one draw needn't show every extreme that they name: `candidates`: the 256 ids of a query are distinct passage ids of its group; only the first counts of them are used. `counts`: some query uses all 256 slots. `owner_map`: each row is a permutation of the group's passage ids.
All inputs are finite; a program needn't handle non-finite values. No bound on the sum of `counts` on one device may be relied on, other than what follows from the above.
Results may differ from the reference program's by a relative error of at most 0.012.
Values may be sent and summed in bfloat16 or wider, within the bound.
A program may use at most 32 MiB of HBM per device.

```python
import math
import jax
import jax.numpy as jnp
import numpy as np
from jax import lax

D = 1024
QUERIES = 24576
POOL = 768
PASSAGES = 6144
CAND = 256
N_GRP = 8


def draw_query_states(key, part):
    key = jax.random.fold_in(key, 11)
    first_key = jax.random.fold_in(key, 0)
    values = jnp.clip(jax.random.normal(first_key, (QUERIES, D), jnp.float32), -6.0, 6.0)
    return values.astype(jnp.bfloat16)


def draw_passage_states(key, part):
    key = jax.random.fold_in(key, 12)
    first_key = jax.random.fold_in(key, 0)
    values = jnp.clip(jax.random.normal(first_key, (PASSAGES, D), jnp.float32), -6.0, 6.0)
    return values.astype(jnp.bfloat16)


def draw_teacher_scores(key, part):
    key = jax.random.fold_in(key, 13)
    first_key = jax.random.fold_in(key, 0)
    values = jnp.clip(2.0 * jax.random.normal(first_key, (QUERIES, CAND), jnp.float32), -8.0, 8.0)
    return values.astype(jnp.float32)


def picks_of(stream_key, rows, number_of, top, lift):
    order = jax.random.permutation(jax.random.fold_in(stream_key, 1), number_of)
    pull = order
    for power in range(3):
        pull = pull * pull // number_of
    pull = pull * lift // number_of
    chance = jax.random.randint(jax.random.fold_in(stream_key, 2), (rows, number_of), 0, 4096) + pull
    fixed_rows = jax.random.permutation(jax.random.fold_in(stream_key, 3), rows)[jnp.arange(number_of) % rows]
    chance = jnp.where(jnp.arange(rows)[:, None] == fixed_rows[None, :], 1 << 14, chance)
    priority = chance * number_of + jnp.arange(number_of)
    return lax.top_k(priority.astype(jnp.int32), top)[1].astype(jnp.int32)


def length_profile(amount, total, most, lean):
    portions = [(1 << 20) // math.isqrt(standing ** lean) + 1 for standing in range(2, amount + 1)]
    surplus, given = total - most - (amount - 1), [1] * (amount - 1)
    while surplus > 0:
        free = [i for i in range(amount - 1) if given[i] < most]
        mass, remaining = sum([portions[i] for i in free]), surplus
        for i in free:
            extra = min(most - given[i], max(1, remaining * portions[i] // mass), surplus)
            given[i] = given[i] + extra
            surplus = surplus - extra
    return np.array([most] + given)


def ragged_sizes(stream_key, amount, total, most, slope):
    if amount == 2:
        one = jax.random.randint(stream_key, (), max(1, total - most), min(most, total - 1) + 1)
        return jnp.stack([one, total - one])
    tallies = jnp.asarray(length_profile(amount, total, most, slope), jnp.int32)
    couples = (amount - 1) // 2
    donor, receiver = tallies[1:1 + 2 * couples:2], tallies[2:2 + 2 * couples:2]
    margin = jnp.minimum(donor - 1, most - receiver)
    moved = jax.random.randint(jax.random.fold_in(stream_key, 1), (couples,), 0, 1 << 20) % (margin + 1)
    tallies = tallies.at[1:1 + 2 * couples:2].set(donor - moved).at[2:2 + 2 * couples:2].set(receiver + moved)
    return tallies[jax.random.permutation(jax.random.fold_in(stream_key, 2), amount)]


def gaussian(rng, shape, width, bound, kind=jnp.bfloat16):
    array = width * jax.random.normal(rng, shape, jnp.float32)
    return jnp.clip(array, min=-bound, max=bound).astype(kind)


def setup_inputs(seed: int = 0) -> dict:
    streams_of = jax.random.split(jax.random.key(seed), 8)
    query_states = draw_query_states(jax.random.fold_in(streams_of[7], 71), 0)
    passage_states = draw_passage_states(jax.random.fold_in(streams_of[7], 71), 0)
    head_weight = gaussian(streams_of[2], (D, D), D ** -0.5, 0.1875)
    candidates = picks_of(streams_of[3], QUERIES, POOL, CAND, 2730)
    counts = ragged_sizes(streams_of[4], QUERIES, QUERIES * CAND * 5 // 8, CAND, 1).astype(jnp.int32)
    teacher_scores = draw_teacher_scores(jax.random.fold_in(streams_of[7], 71), 0)
    owner_map = jax.vmap(lambda own: jax.random.permutation(own, POOL))(jax.random.split(streams_of[6], N_GRP)).reshape((N_GRP, POOL)).astype(jnp.int32)
    return dict(query_states=query_states, passage_states=passage_states, head_weight=head_weight, candidates=candidates, counts=counts, teacher_scores=teacher_scores, owner_map=owner_map)


def masked_softmax(values, valid_mask):
    masked = jnp.where(valid_mask, values, -jnp.inf)
    row_top = jnp.max(masked, axis=1, keepdims=True)
    weights = jnp.exp(jnp.where(valid_mask, values - row_top, -jnp.inf))
    return weights / jnp.sum(weights, axis=1, keepdims=True)


def reference(query_states, passage_states, head_weight, candidates, counts, teacher_scores, owner_map):
    score_scale = D ** -0.5
    query_proj = jnp.dot(query_states, head_weight, preferred_element_type=jnp.float32).astype(jnp.bfloat16)
    passage_proj = jnp.dot(passage_states, head_weight, preferred_element_type=jnp.float32).astype(jnp.bfloat16)
    group_rows = QUERIES // N_GRP

    def one_group(inputs):
        query_rows, passage_rows, cand_rows, count_rows, teacher_rows, owner_row = inputs
        scores_full = score_scale * lax.dot_general(query_rows, passage_rows, (((1,), (1,)), ((), ())), preferred_element_type=jnp.float32)
        slot_ids = jnp.take(owner_row, cand_rows, axis=0).astype(jnp.int32)
        score = jnp.take_along_axis(scores_full, slot_ids, axis=1)
        valid_mask = jnp.arange(CAND, dtype=jnp.int32)[None, :] < count_rows[:, None]
        student = masked_softmax(score, valid_mask)
        teacher = masked_softmax(teacher_rows, valid_mask)
        dscore = jnp.where(valid_mask, 256.0 * (student - teacher), 0.0).astype(jnp.bfloat16)
        row_index = jnp.arange(group_rows, dtype=jnp.int32)[:, None]
        dense_grad = jnp.zeros((group_rows, POOL), jnp.float32).at[row_index, slot_ids].add(dscore.astype(jnp.float32)).astype(jnp.bfloat16)
        grad_query = (score_scale * jnp.dot(dense_grad, passage_rows, preferred_element_type=jnp.float32)).astype(jnp.bfloat16)
        grad_passage = (score_scale * lax.dot_general(dense_grad, query_rows, (((0,), (0,)), ((), ())), preferred_element_type=jnp.float32)).astype(jnp.bfloat16)
        return grad_query, grad_passage

    grad_query, grad_passage = lax.map(one_group, (
        query_proj.reshape(N_GRP, group_rows, D),
        passage_proj.reshape(N_GRP, POOL, D),
        candidates.reshape(N_GRP, group_rows, CAND),
        counts.reshape(N_GRP, group_rows),
        teacher_scores.reshape(N_GRP, group_rows, CAND),
        owner_map))
    grad_query = grad_query.reshape(QUERIES, D)
    grad_passage = grad_passage.reshape(PASSAGES, D)
    query_grad = lax.dot_general(grad_query, head_weight, (((1,), (1,)), ((), ())), preferred_element_type=jnp.float32).astype(jnp.bfloat16)
    passage_grad = lax.dot_general(grad_passage, head_weight, (((1,), (1,)), ((), ())), preferred_element_type=jnp.float32).astype(jnp.bfloat16)
    head_grad = lax.dot_general(query_states, grad_query, (((0,), (0,)), ((), ())), preferred_element_type=jnp.float32)
    head_grad = head_grad + lax.dot_general(passage_states, grad_passage, (((0,), (0,)), ((), ())), preferred_element_type=jnp.float32)
    return query_grad, passage_grad, head_grad
```

```python
import functools

import jax
import jax.numpy as jnp
from jax import lax
from jax.experimental import pallas as pl
from jax.experimental.pallas import tpu as pltpu
from jax.sharding import PartitionSpec as P

MESH = pl.DeviceIdType.MESH
NG, NZ, NY = 8, 12, 8
ROWS, OWN, D, CAND, POOL = 32, 8, 1024, 256, 768
QB = NY * ROWS
PB = 128
HALF = D // 2
OUT_ROWS = D // NG
ROW_PIECE = OUT_ROWS // NY
N_COL = D // 128
BF, F32 = jnp.bfloat16, jnp.float32
FAR = -1.0e30


def dot(a, b, ca, cb):
    return lax.dot_general(a, b, (((ca,), (cb,)), ((), ())), preferred_element_type=F32)


def fold(rows):
    return jnp.concatenate([rows[:, :, :HALF], rows[:, :, HALF:]], axis=1).astype(BF)


def unfold(block):
    wide = block.astype(F32)
    wide = jnp.concatenate([wide[:, :OWN, :], wide[:, OWN:, :]], axis=2)
    return wide.reshape(wide.shape[0] * OWN, D)


class Exchange:
    def __init__(self, n, me, device, send_sem, recv_sem):
        self.n, self.me, self.device = n, me, device
        self.send_sem, self.recv_sem = send_sem, recv_sem

    def copy(self, k, src, dst):
        peer = lax.rem(self.me + k, self.n)
        return pltpu.make_async_remote_copy(
            src_ref=src(peer),
            dst_ref=dst(self.me),
            send_sem=self.send_sem.at[k - 1],
            recv_sem=self.recv_sem.at[k - 1],
            device_id=self.device(peer),
            device_id_type=MESH,
        )

    def arrival(self, k, dst):
        sender = lax.rem(self.me + self.n - k, self.n)
        return pltpu.make_async_remote_copy(
            src_ref=dst(sender),
            dst_ref=dst(sender),
            send_sem=self.send_sem.at[k - 1],
            recv_sem=self.recv_sem.at[k - 1],
            device_id=self.device(sender),
            device_id_type=MESH,
        )

    def each(self, body):
        def step(k, carry):
            body(k)
            return carry

        lax.fori_loop(1, self.n, step, 0)

    def start(self, src, dst):
        self.each(lambda k: self.copy(k, src, dst).start())

    def wait_recv(self, dst):
        self.each(lambda k: self.arrival(k, dst).wait_recv())

    def wait_send(self, src, dst):
        self.each(lambda k: self.copy(k, src, dst).wait_send())


def kernel(
    qs_hbm, ps_hbm, w_hbm, cand_hbm, counts_hbm, teach_hbm, own_hbm,
    qgrad_ref, pgrad_ref, head_ref,
    qs_all, ps_all, pg_all, t_all, st_all, v_in, u_in, vg_all, h_in, hz_in, hz_all, h_all,
    ps_loc, ps_mine, w_ref, cand_ref, counts_ref, teach_ref, own_ref,
    b_ref, y_ref, parts_ref, tb_ref, t_out, st_out, v_out, u_out, h_out, hz_out,
    q_ref, p128_ref, ps128_ref, p64_ref, ps64_ref, v64_ref, vw_ref,
    local_sem, ysend, yrecv, zsend, zrecv, gsend, grecv,
):
    g = lax.axis_index("grp")
    d = lax.axis_index("dev")
    z, y = d // NY, lax.rem(d, NY)
    scale = D ** -0.5

    def on_y(i):
        return (g, z * NY + i)

    def on_z(i):
        return (g, i * NY + y)

    def on_g(i):
        return (i, d)

    def y_axis(s):
        return Exchange(NY, y, on_y, ysend.at[s], yrecv.at[s])

    def z_axis(s):
        return Exchange(NZ, z, on_z, zsend.at[s], zrecv.at[s])

    def g_axis(s):
        return Exchange(NG, g, on_g, gsend.at[s], grecv.at[s])

    barrier = pltpu.get_barrier_semaphore()
    for n, me, device in ((NZ, z, on_z), (NY, y, on_y), (NG, g, on_g)):
        def greet(k, carry, n=n, me=me, device=device):
            pl.semaphore_signal(
                barrier, inc=1, device_id=device(lax.rem(me + k, n)), device_id_type=MESH
            )
            return carry

        lax.fori_loop(1, n, greet, 0)

    locals_ = [
        pltpu.make_async_copy(src, dst, local_sem.at[i])
        for i, (src, dst) in enumerate(
            [
                (cand_hbm, cand_ref),
                (own_hbm, own_ref),
                (counts_hbm, counts_ref),
                (teach_hbm, teach_ref),
                (ps_hbm, ps_loc),
                (qs_hbm, qs_all.at[y]),
                (w_hbm, w_ref),
            ]
        )
    ]
    for copy in locals_:
        copy.start()
    for copy in locals_[:5]:
        copy.wait()

    mine = fold(ps_loc[...].astype(F32)[None])
    ps_mine[...] = mine
    ps_all[pl.ds(z, 1)] = mine
    pg_all[pl.ds(g, 1)] = mine

    row_id = lax.broadcasted_iota(jnp.int32, (ROWS, 128), 0)
    lane_id = lax.broadcasted_iota(jnp.int32, (ROWS, 128), 1)
    limit = jnp.zeros((ROWS, 128), jnp.int32)
    for i in range(ROWS):
        limit = jnp.where(row_id == i, counts_ref[i], limit)
    storage = []
    for c in range(CAND // 128):
        ids = cand_ref[:, c * 128 : (c + 1) * 128]
        low, high = ids & 127, ids >> 7
        row = jnp.zeros((ROWS, 128), jnp.int32)
        for t in range(POOL // 128):
            table = jnp.broadcast_to(own_ref[:, t * 128 : (t + 1) * 128], (ROWS, 128))
            picked = jnp.take_along_axis(table, low, axis=1, mode="promise_in_bounds")
            row = jnp.where(high == t, picked, row)
        storage.append(row)
    storage = jnp.concatenate(storage, axis=1)
    b_ref[...] = ((storage >> 6) << 3) | (storage & 7)
    y_ref[...] = (storage >> 3) & 7
    slot_id = jnp.concatenate([lane_id, lane_id + 128], axis=1)
    valid = slot_id < jnp.concatenate([limit, limit], axis=1)
    values = teach_ref[...]
    top = jnp.max(jnp.where(valid, values, -jnp.inf), axis=1, keepdims=True)
    weights = jnp.where(valid, jnp.exp(jnp.where(valid, values - top, 0.0)), 0.0)
    teacher = weights / jnp.sum(weights, axis=1, keepdims=True)
    part = teacher.astype(BF).astype(F32)
    parts_ref[0] = part
    rest = teacher - part
    part = rest.astype(BF).astype(F32)
    parts_ref[1] = part
    parts_ref[2] = rest - part
    parts_ref[3] = jnp.where(valid, 1.0, 0.0)

    pl.semaphore_wait(barrier, NZ + NY + NG - 3)

    locals_[5].wait()
    gather_q, gather_p, gather_pg = y_axis(0), z_axis(0), g_axis(0)
    gather_q.start(lambda i: qs_all.at[y], lambda i: qs_all.at[i])
    gather_p.start(lambda i: ps_mine.at[0], lambda i: ps_all.at[i])
    gather_pg.start(lambda i: ps_mine.at[0], lambda i: pg_all.at[i])

    block_id = lax.broadcasted_iota(jnp.int32, (PB, CAND), 0)
    owner_id = lax.broadcasted_iota(jnp.int32, (NY, CAND), 0)

    def densify(i, carry):
        hot = jnp.where(block_id == b_ref[pl.ds(i, 1), :], 1.0, 0.0).astype(BF)
        mask = owner_id == y_ref[pl.ds(i, 1), :]
        lhs = jnp.concatenate(
            [jnp.where(mask, parts_ref[n, pl.ds(i, 1), :], 0.0) for n in range(4)], axis=0
        ).astype(BF)
        out = dot(lhs, hot, 1, 1)
        dense = out[0:8] + (out[8:16] + out[16:24])
        tb_ref[pl.ds(pl.multiple_of(i * NY, NY), NY), :] = jnp.where(out[24:32] > 0.5, dense, -1.0)
        return carry

    lax.fori_loop(0, ROWS, densify, 0, unroll=4)
    for i in range(NY):
        t_out[i] = tb_ref[pl.ds(i, ROWS, stride=NY), :]
    t_all[pl.ds(y, 1)] = t_out[pl.ds(y, 1)]
    gather_t = y_axis(1)
    gather_t.start(lambda i: t_out.at[i], lambda i: t_all.at[i])

    locals_[6].wait()
    gather_p.wait_recv(lambda i: ps_all.at[i])
    gather_pg.wait_recv(lambda i: pg_all.at[i])
    ps128_ref[...] = jnp.concatenate(
        [unfold(ps_all[...]), jnp.zeros((PB - NZ * OWN, D), F32)], axis=0
    ).astype(BF)
    ps64_ref[...] = unfold(pg_all[...])
    p128_ref[...] = dot(ps128_ref[...], w_ref[...], 1, 0).astype(BF)
    p64_ref[...] = dot(ps64_ref[...].astype(BF), w_ref[...], 1, 0).astype(BF)
    gather_q.wait_recv(lambda i: qs_all.at[i])
    qs_block = qs_all[...].reshape(QB, D)
    q_ref[...] = dot(qs_block, w_ref[...], 1, 0).astype(BF)

    score = scale * dot(p128_ref[...], q_ref[...], 1, 1)
    gather_t.wait_recv(lambda i: t_all.at[i])
    teach = t_all[...].reshape(QB, PB).T
    used = teach >= 0.0
    local_top = jnp.max(jnp.where(used, score, FAR), axis=0, keepdims=True)
    expo = jnp.where(used, jnp.exp(jnp.where(used, score - local_top, 0.0)), 0.0)
    local_sum = jnp.sum(expo, axis=0, keepdims=True)
    stats = jnp.where(
        lax.broadcasted_iota(jnp.int32, (8, QB), 0) == 0, local_top, local_sum
    )
    st_out[...] = stats
    st_all[pl.ds(y, 1)] = stats[None]
    stats_x = y_axis(2)
    stats_x.start(lambda i: st_out, lambda i: st_all.at[i])
    stats_x.wait_recv(lambda i: st_all.at[i])
    tops = st_all[:, 0:1, :]
    top = jnp.max(tops, axis=0)
    total = jnp.sum(st_all[:, 1:2, :] * jnp.exp(tops - top[None]), axis=0)
    student = expo * (jnp.exp(local_top - top) / total)
    dscore = jnp.where(used, 256.0 * (student - teach), 0.0).astype(BF)

    v_part = scale * dot(dscore, qs_block, 1, 0)
    v_out[...] = fold(v_part[: NZ * OWN].reshape(NZ, OWN, D))
    v_in[pl.ds(z, 1)] = v_out[pl.ds(z, 1)]
    reduce_v = z_axis(1)
    reduce_v.start(lambda i: v_out.at[i], lambda i: v_in.at[i])
    u_part = scale * dot(dscore.astype(F32).T.astype(BF), ps128_ref[...], 1, 0)
    u_out[...] = u_part.astype(BF).reshape(NY, ROWS, D)
    u_in[pl.ds(y, 1)] = u_out[pl.ds(y, 1)]
    reduce_u = y_axis(3)
    reduce_u.start(lambda i: u_out.at[i], lambda i: u_in.at[i])

    reduce_v.wait_recv(lambda i: v_in.at[i])
    v_sum = jnp.sum(v_in[...].astype(F32), axis=0)
    vg_all[pl.ds(g, 1)] = v_sum.astype(BF)[None]
    gather_v = g_axis(1)
    gather_v.start(lambda i: vg_all.at[g], lambda i: vg_all.at[i])
    gather_v.wait_recv(lambda i: vg_all.at[i])
    v64_ref[...] = unfold(vg_all[...])
    vw = dot(v64_ref[...].astype(BF), w_ref[...], 1, 0).astype(BF)
    vw_ref[...] = vw.astype(F32)
    cols = pl.ds(pl.multiple_of(g * OUT_ROWS, OUT_ROWS), OUT_ROWS)
    left = jnp.concatenate([v64_ref[:, cols], ps64_ref[:, cols]], axis=0).T.astype(BF)
    right = jnp.concatenate([p64_ref[...], vw], axis=0)
    h_out[...] = dot(left, right, 1, 0).astype(BF).reshape(NY, ROW_PIECE, D)
    h_in[pl.ds(y, 1)] = h_out[pl.ds(y, 1)]
    reduce_h = y_axis(4)
    reduce_h.start(lambda i: h_out.at[i], lambda i: h_in.at[i])

    reduce_u.wait_recv(lambda i: u_in.at[i])
    u_sum = jnp.sum(u_in[...].astype(F32), axis=0).astype(BF)
    gq = dot(u_sum, w_ref[...], 1, 0)
    gp = vw_ref[pl.ds(pl.multiple_of(g * OWN, OWN), OWN), :]
    rows = jnp.concatenate([gq, gp, gp], axis=0).astype(BF)
    grads = dot(rows, w_ref[...], 1, 1)
    qgrad_ref[...] = grads[:ROWS].astype(BF)
    pgrad_ref[...] = grads[ROWS : ROWS + OWN].astype(BF)

    reduce_h.wait_recv(lambda i: h_in.at[i])
    h_sum = jnp.sum(h_in[...].astype(F32), axis=0).astype(BF)
    for i in range(N_COL):
        hz_out[i] = h_sum[:, i * 128 : (i + 1) * 128]
    reduce_hz, gather_hz = z_axis(2), z_axis(3)

    def send_piece(k):
        @pl.when(lax.rem(z + k, NZ) < N_COL)
        def _():
            reduce_hz.copy(
                k, lambda i: hz_out.at[lax.rem(i, N_COL)], lambda i: hz_in.at[i]
            ).start()

    reduce_hz.each(send_piece)

    @pl.when(z < N_COL)
    def _():
        spot = lax.rem(z, N_COL)
        hz_in[pl.ds(z, 1)] = hz_out[pl.ds(spot, 1)]
        reduce_hz.wait_recv(lambda i: hz_in.at[i])
        hz_all[pl.ds(spot, 1)] = jnp.sum(hz_in[...].astype(F32), axis=0).astype(BF)[None]
        gather_hz.start(lambda i: hz_all.at[spot], lambda i: hz_all.at[lax.rem(i, N_COL)])

    def take_piece(k):
        @pl.when(lax.rem(z + NZ - k, NZ) < N_COL)
        def _():
            gather_hz.arrival(k, lambda i: hz_all.at[lax.rem(i, N_COL)]).wait_recv()

    gather_hz.each(take_piece)
    h_all[pl.ds(y, 1)] = hz_all[...][None]
    gather_h = y_axis(5)
    gather_h.start(lambda i: hz_all, lambda i: h_all.at[i])
    gather_h.wait_recv(lambda i: h_all.at[i])
    for r in range(NY):
        for c in range(N_COL):
            head_ref[r * ROW_PIECE : (r + 1) * ROW_PIECE, c * 128 : (c + 1) * 128] = h_all[
                r, c
            ].astype(F32)

    gather_q.wait_send(lambda i: qs_all.at[y], lambda i: qs_all.at[i])
    gather_p.wait_send(lambda i: ps_mine.at[0], lambda i: ps_all.at[i])
    gather_pg.wait_send(lambda i: ps_mine.at[0], lambda i: pg_all.at[i])
    gather_t.wait_send(lambda i: t_out.at[i], lambda i: t_all.at[i])
    stats_x.wait_send(lambda i: st_out, lambda i: st_all.at[i])
    reduce_v.wait_send(lambda i: v_out.at[i], lambda i: v_in.at[i])
    reduce_u.wait_send(lambda i: u_out.at[i], lambda i: u_in.at[i])
    gather_v.wait_send(lambda i: vg_all.at[g], lambda i: vg_all.at[i])
    reduce_h.wait_send(lambda i: h_out.at[i], lambda i: h_in.at[i])

    def sent_piece(k):
        @pl.when(lax.rem(z + k, NZ) < N_COL)
        def _():
            reduce_hz.copy(
                k, lambda i: hz_out.at[lax.rem(i, N_COL)], lambda i: hz_in.at[i]
            ).wait_send()

    reduce_hz.each(sent_piece)

    @pl.when(z < N_COL)
    def _():
        spot = lax.rem(z, N_COL)
        gather_hz.wait_send(lambda i: hz_all.at[spot], lambda i: hz_all.at[lax.rem(i, N_COL)])

    gather_h.wait_send(lambda i: hz_all, lambda i: h_all.at[i])


def shards(
    query_states, passage_states, head_weight, candidates, counts, teacher_scores, owner_map
):
    vmem = pltpu.VMEM
    scratch = [
        vmem((NY, ROWS, D), BF),
        vmem((NZ, 16, HALF), BF),
        vmem((NG, 16, HALF), BF),
        vmem((NY, ROWS, PB), F32),
        vmem((NY, 8, QB), F32),
        vmem((NZ, 16, HALF), BF),
        vmem((NY, ROWS, D), BF),
        vmem((NG, 16, HALF), BF),
        vmem((NY, ROW_PIECE, D), BF),
        vmem((NZ, ROW_PIECE, 128), BF),
        vmem((N_COL, ROW_PIECE, 128), BF),
        vmem((NY, N_COL, ROW_PIECE, 128), BF),
        vmem((OWN, D), BF),
        vmem((1, 16, HALF), BF),
        vmem((D, D), BF),
        vmem((ROWS, CAND), jnp.int32),
        pltpu.SMEM((ROWS,), jnp.int32),
        vmem((ROWS, CAND), F32),
        vmem((1, POOL), jnp.int32),
        vmem((ROWS, CAND), jnp.int32),
        vmem((ROWS, CAND), jnp.int32),
        vmem((4, ROWS, CAND), F32),
        vmem((ROWS * NY, PB), F32),
        vmem((NY, ROWS, PB), F32),
        vmem((8, QB), F32),
        vmem((NZ, 16, HALF), BF),
        vmem((NY, ROWS, D), BF),
        vmem((NY, ROW_PIECE, D), BF),
        vmem((N_COL, ROW_PIECE, 128), BF),
        vmem((QB, D), BF),
        vmem((PB, D), BF),
        vmem((PB, D), BF),
        vmem((NG * OWN, D), BF),
        vmem((NG * OWN, D), F32),
        vmem((NG * OWN, D), F32),
        vmem((NG * OWN, D), F32),
        pltpu.SemaphoreType.DMA((7,)),
        pltpu.SemaphoreType.DMA((6, NY - 1)),
        pltpu.SemaphoreType.DMA((6, NY - 1)),
        pltpu.SemaphoreType.DMA((4, NZ - 1)),
        pltpu.SemaphoreType.DMA((4, NZ - 1)),
        pltpu.SemaphoreType.DMA((2, NG - 1)),
        pltpu.SemaphoreType.DMA((2, NG - 1)),
    ]
    return pl.pallas_call(
        kernel,
        out_shape=(
            jax.ShapeDtypeStruct((ROWS, D), BF),
            jax.ShapeDtypeStruct((OWN, D), BF),
            jax.ShapeDtypeStruct((OUT_ROWS, D), F32),
        ),
        in_specs=[pl.BlockSpec(memory_space=pltpu.HBM)] * 7,
        out_specs=tuple([pl.BlockSpec(memory_space=vmem)] * 3),
        scratch_shapes=scratch,
        name="distill",
        compiler_params=pltpu.CompilerParams(
            collective_id=0, has_side_effects=True, vmem_limit_bytes=61 * 1024 * 1024
        ),
    )(query_states, passage_states, head_weight, candidates, counts, teacher_scores, owner_map)


def solution(mesh):
    rows = P(("grp", "dev"), None)
    in_specs = (rows, rows, P(), rows, P(("grp", "dev")), rows, P("grp", None))
    out_specs = (rows, rows, P("grp", None))
    return jax.shard_map(shards, mesh=mesh, in_specs=in_specs, out_specs=out_specs, check_vma=False)
```

```python
import functools

import jax
import jax.numpy as jnp
from jax import lax
from jax.experimental import pallas as pl
from jax.experimental.pallas import tpu as pltpu
from jax.sharding import PartitionSpec as P

MESH = pl.DeviceIdType.MESH
NG, NZ, NY = 8, 12, 8
ROWS, OWN, D, CAND, POOL = 32, 8, 1024, 256, 768
QB = NY * ROWS
PB = 128
HALF = D // 2
OUT_ROWS = D // NG
ROW_PIECE = OUT_ROWS // NY
N_COL = D // 128
HALF_COL = N_COL // 2
BF, F32 = jnp.bfloat16, jnp.float32
FAR = -1.0e30
Q_ORDER = (0, 4, 3, 5, 2, 6, 1, 7)


def dot(a, b, ca, cb):
    return lax.dot_general(a, b, (((ca,), (cb,)), ((), ())), preferred_element_type=F32)


def fold(rows):
    return jnp.concatenate([rows[:, :, :HALF], rows[:, :, HALF:]], axis=1).astype(BF)


def unfold(block):
    wide = block.astype(F32)
    wide = jnp.concatenate([wide[:, :OWN, :], wide[:, OWN:, :]], axis=2)
    return wide.reshape(wide.shape[0] * OWN, D)


class Exchange:
    def __init__(self, n, me, device, send_sem, recv_sem):
        self.n, self.me, self.device = n, me, device
        self.send_sem, self.recv_sem = send_sem, recv_sem

    def copy(self, k, src, dst):
        peer = lax.rem(self.me + k, self.n)
        return pltpu.make_async_remote_copy(
            src_ref=src(peer),
            dst_ref=dst(self.me),
            send_sem=self.send_sem.at[k - 1],
            recv_sem=self.recv_sem.at[k - 1],
            device_id=self.device(peer),
            device_id_type=MESH,
        )

    def arrival(self, k, dst):
        sender = lax.rem(self.me + self.n - k, self.n)
        return pltpu.make_async_remote_copy(
            src_ref=dst(sender),
            dst_ref=dst(sender),
            send_sem=self.send_sem.at[k - 1],
            recv_sem=self.recv_sem.at[k - 1],
            device_id=self.device(sender),
            device_id_type=MESH,
        )

    def each(self, body):
        def step(k, carry):
            body(k)
            return carry

        lax.fori_loop(1, self.n, step, 0)

    def far_first(self, body):
        for k in sorted(range(1, self.n), key=lambda k: -min(k, self.n - k)):
            body(k)

    def start(self, src, dst):
        self.far_first(lambda k: self.copy(k, src, dst).start())
        return lambda: self.each(lambda k: self.copy(k, src, dst).wait_send())

    def wait_recv(self, dst):
        self.each(lambda k: self.arrival(k, dst).wait_recv())


def kernel(
    qs_hbm, ps_hbm, w_hbm, cand_hbm, counts_hbm, teach_hbm, own_hbm,
    qgrad_ref, pgrad_ref, head_ref,
    qs_all, ps_all, pg_all, t_all, st_all, v_in, u_in, vg_all, h_in, hz_in, hz_all, h_all,
    ps_loc, ps_mine, w_ref, cand_ref, counts_ref, teach_ref, own_ref,
    b_ref, y_ref, parts_ref, tb_ref, t_out, st_out, v_out, u_out, h_out, hz_out,
    q_ref, p128_ref, ps128_ref, p64_ref, ps64_ref, v64_ref, vw_ref,
    local_sem, ysend, yrecv, zsend, zrecv, gsend, grecv,
):
    g = lax.axis_index("grp")
    d = lax.axis_index("dev")
    z, y = d // NY, lax.rem(d, NY)
    scale = D ** -0.5

    def on_y(i):
        return (g, z * NY + i)

    def on_z(i):
        return (g, i * NY + y)

    def on_g(i):
        return (i, d)

    def y_axis(s):
        return Exchange(NY, y, on_y, ysend.at[s], yrecv.at[s])

    def z_axis(s):
        return Exchange(NZ, z, on_z, zsend.at[s], zrecv.at[s])

    def g_axis(s):
        return Exchange(NG, g, on_g, gsend.at[s], grecv.at[s])

    sends = []

    barrier = pltpu.get_barrier_semaphore()
    for n, me, device in ((NZ, z, on_z), (NY, y, on_y), (NG, g, on_g)):
        def greet(k, carry, n=n, me=me, device=device):
            pl.semaphore_signal(
                barrier, inc=1, device_id=device(lax.rem(me + k, n)), device_id_type=MESH
            )
            return carry

        lax.fori_loop(1, n, greet, 0)

    locals_ = [
        pltpu.make_async_copy(src, dst, local_sem.at[i])
        for i, (src, dst) in enumerate(
            [
                (ps_hbm, ps_loc),
                (qs_hbm, qs_all.at[y]),
                (cand_hbm, cand_ref),
                (own_hbm, own_ref),
                (counts_hbm, counts_ref),
                (teach_hbm, teach_ref),
                (w_hbm, w_ref),
            ]
        )
    ]
    for copy in locals_:
        copy.start()
    locals_[0].wait()
    mine = fold(ps_loc[...].astype(F32)[None])
    ps_mine[...] = mine
    ps_all[pl.ds(z, 1)] = mine
    pg_all[pl.ds(g, 1)] = mine
    locals_[1].wait()

    pl.semaphore_wait(barrier, NZ + NY + NG - 3)
    gather_q, gather_p, gather_pg = y_axis(0), z_axis(0), g_axis(0)
    sends.append(gather_q.start(lambda i: qs_all.at[y], lambda i: qs_all.at[i]))
    sends.append(gather_p.start(lambda i: ps_mine.at[0], lambda i: ps_all.at[i]))
    sends.append(gather_pg.start(lambda i: ps_mine.at[0], lambda i: pg_all.at[i]))

    for copy in locals_[2:6]:
        copy.wait()
    row_id = lax.broadcasted_iota(jnp.int32, (ROWS, 128), 0)
    lane_id = lax.broadcasted_iota(jnp.int32, (ROWS, 128), 1)
    limit = jnp.zeros((ROWS, 128), jnp.int32)
    for i in range(ROWS):
        limit = jnp.where(row_id == i, counts_ref[i], limit)
    storage = []
    for c in range(CAND // 128):
        ids = cand_ref[:, c * 128 : (c + 1) * 128]
        low, high = ids & 127, ids >> 7
        row = jnp.zeros((ROWS, 128), jnp.int32)
        for t in range(POOL // 128):
            table = jnp.broadcast_to(own_ref[:, t * 128 : (t + 1) * 128], (ROWS, 128))
            picked = jnp.take_along_axis(table, low, axis=1, mode="promise_in_bounds")
            row = jnp.where(high == t, picked, row)
        storage.append(row)
    storage = jnp.concatenate(storage, axis=1)
    b_ref[...] = ((storage >> 6) << 3) | (storage & 7)
    y_ref[...] = (storage >> 3) & 7
    slot_id = jnp.concatenate([lane_id, lane_id + 128], axis=1)
    valid = slot_id < jnp.concatenate([limit, limit], axis=1)
    values = teach_ref[...]
    top = jnp.max(jnp.where(valid, values, -jnp.inf), axis=1, keepdims=True)
    weights = jnp.where(valid, jnp.exp(jnp.where(valid, values - top, 0.0)), 0.0)
    teacher = weights / jnp.sum(weights, axis=1, keepdims=True)
    part = teacher.astype(BF).astype(F32)
    parts_ref[0] = part
    rest = teacher - part
    part = rest.astype(BF).astype(F32)
    parts_ref[1] = part
    parts_ref[2] = rest - part
    parts_ref[3] = jnp.where(valid, 1.0, 0.0)

    block_id = lax.broadcasted_iota(jnp.int32, (PB, CAND), 0)
    owner_id = lax.broadcasted_iota(jnp.int32, (NY, CAND), 0)

    def densify(i, carry):
        hot = jnp.where(block_id == b_ref[pl.ds(i, 1), :], 1.0, 0.0).astype(BF)
        mask = owner_id == y_ref[pl.ds(i, 1), :]
        lhs = jnp.concatenate(
            [jnp.where(mask, parts_ref[n, pl.ds(i, 1), :], 0.0) for n in range(4)], axis=0
        ).astype(BF)
        out = dot(lhs, hot, 1, 1)
        dense = out[0:8] + (out[8:16] + out[16:24])
        tb_ref[pl.ds(pl.multiple_of(i * NY, NY), NY), :] = jnp.where(out[24:32] > 0.5, dense, -1.0)
        return carry

    lax.fori_loop(0, ROWS, densify, 0, unroll=4)
    for i in range(NY):
        t_out[i] = tb_ref[pl.ds(i, ROWS, stride=NY), :]
    t_all[pl.ds(y, 1)] = t_out[pl.ds(y, 1)]
    gather_t = y_axis(1)
    sends.append(gather_t.start(lambda i: t_out.at[i], lambda i: t_all.at[i]))


    locals_[6].wait()
    gather_p.wait_recv(lambda i: ps_all.at[i])
    gather_pg.wait_recv(lambda i: pg_all.at[i])
    ps128_ref[...] = jnp.concatenate(
        [unfold(ps_all[...]), jnp.zeros((PB - NZ * OWN, D), F32)], axis=0
    ).astype(BF)
    ps64_ref[...] = unfold(pg_all[...])
    p128_ref[...] = dot(ps128_ref[...], w_ref[...], 1, 0).astype(BF)
    p64_ref[...] = dot(ps64_ref[...].astype(BF), w_ref[...], 1, 0).astype(BF)
    for part in (Q_ORDER[:4], Q_ORDER[4:]):
        spots = []
        for k in part:
            if k:
                gather_q.arrival(k, lambda i: qs_all.at[i]).wait_recv()
            spots.append(lax.rem(y + NY - k, NY))
        some = jnp.concatenate([qs_all[pl.ds(i, 1)] for i in spots], axis=0)
        done = dot(some.reshape(4 * ROWS, D), w_ref[...], 1, 0).astype(BF)
        for n, i in enumerate(spots):
            q_ref[pl.ds(i, 1)] = done[n * ROWS : (n + 1) * ROWS][None]
    qs_block = qs_all[...].reshape(QB, D)


    score = scale * dot(p128_ref[...], q_ref[...].reshape(QB, D), 1, 1)
    gather_t.wait_recv(lambda i: t_all.at[i])
    teach = t_all[...].reshape(QB, PB).T
    used = teach >= 0.0
    local_top = jnp.max(jnp.where(used, score, FAR), axis=0, keepdims=True)
    expo = jnp.where(used, jnp.exp(jnp.where(used, score - local_top, 0.0)), 0.0)
    local_sum = jnp.sum(expo, axis=0, keepdims=True)
    stats = jnp.where(
        lax.broadcasted_iota(jnp.int32, (8, QB), 0) == 0, local_top, local_sum
    )
    st_out[...] = stats
    st_all[pl.ds(y, 1)] = stats[None]
    stats_x = y_axis(2)
    sends.append(stats_x.start(lambda i: st_out, lambda i: st_all.at[i]))
    stats_x.wait_recv(lambda i: st_all.at[i])
    tops = st_all[:, 0:1, :]
    top = jnp.max(tops, axis=0)
    total = jnp.sum(st_all[:, 1:2, :] * jnp.exp(tops - top[None]), axis=0)
    student = expo * (jnp.exp(local_top - top) / total)
    dscore = jnp.where(used, 256.0 * (student - teach), 0.0).astype(BF)


    v_part = scale * dot(dscore, qs_block, 1, 0)
    v_out[...] = fold(v_part[: NZ * OWN].reshape(NZ, OWN, D))
    v_in[pl.ds(z, 1)] = v_out[pl.ds(z, 1)]
    reduce_v = z_axis(1)
    sends.append(reduce_v.start(lambda i: v_out.at[i], lambda i: v_in.at[i]))
    u_part = scale * dot(dscore.astype(F32).T.astype(BF), ps128_ref[...], 1, 0)
    u_out[...] = u_part.astype(BF).reshape(NY, ROWS, D)
    u_in[pl.ds(y, 1)] = u_out[pl.ds(y, 1)]
    reduce_u = y_axis(3)
    sends.append(reduce_u.start(lambda i: u_out.at[i], lambda i: u_in.at[i]))


    reduce_v.wait_recv(lambda i: v_in.at[i])
    v_sum = jnp.sum(v_in[...].astype(F32), axis=0)
    vg_all[pl.ds(g, 1)] = v_sum.astype(BF)[None]
    gather_v = g_axis(1)
    sends.append(gather_v.start(lambda i: vg_all.at[g], lambda i: vg_all.at[i]))
    gather_v.wait_recv(lambda i: vg_all.at[i])
    v64_ref[...] = unfold(vg_all[...])
    cols = pl.ds(pl.multiple_of(g * OUT_ROWS, OUT_ROWS), OUT_ROWS)
    left = jnp.concatenate([v64_ref[:, cols], ps64_ref[:, cols]], axis=0).T.astype(BF)
    v64 = v64_ref[...].astype(BF)
    reduce_h = []
    for h in range(2):
        half = slice(h * HALF, (h + 1) * HALF)
        vw = dot(v64, w_ref[:, half], 1, 0).astype(BF)
        vw_ref[:, half] = vw.astype(F32)
        right = jnp.concatenate([p64_ref[:, half], vw], axis=0)
        h_out[:, h] = dot(left, right, 1, 0).astype(BF).reshape(NY, ROW_PIECE, HALF)
        h_in[pl.ds(y, 1), h] = h_out[pl.ds(y, 1), h]
        reduce_h.append(y_axis(4 + h))
        sends.append(
            reduce_h[h].start(lambda i, h=h: h_out.at[i, h], lambda i, h=h: h_in.at[i, h])
        )

    reduce_u.wait_recv(lambda i: u_in.at[i])
    u_sum = jnp.sum(u_in[...].astype(F32), axis=0).astype(BF)
    gq = dot(u_sum, w_ref[...], 1, 0)
    gp = vw_ref[pl.ds(pl.multiple_of(g * OWN, OWN), OWN), :]
    rows = jnp.concatenate([gq, gp, gp], axis=0).astype(BF)
    grads = dot(rows, w_ref[...], 1, 1)
    qgrad_ref[...] = grads[:ROWS].astype(BF)
    pgrad_ref[...] = grads[ROWS : ROWS + OWN].astype(BF)


    reduce_hz, gather_hz = z_axis(2), z_axis(3)
    for h in range(2):
        reduce_h[h].wait_recv(lambda i: h_in.at[i, h])
        h_sum = jnp.sum(h_in[:, h].astype(F32), axis=0).astype(BF)
        for i in range(HALF_COL):
            hz_out[h * HALF_COL + i] = h_sum[:, i * 128 : (i + 1) * 128]

        def owner(k, h=h):
            return lax.div(lax.rem(z + k, NZ), HALF_COL) == h

        def piece(k):
            return reduce_hz.copy(
                k, lambda i: hz_out.at[lax.rem(i, N_COL)], lambda i: hz_in.at[i]
            )

        def send_piece(k, owner=owner):
            @pl.when(owner(k))
            def _():
                piece(k).start()

        def sent_piece(k, owner=owner):
            @pl.when(owner(k))
            def _():
                piece(k).wait_send()

        reduce_hz.far_first(send_piece)
        sends.append(lambda sent_piece=sent_piece: reduce_hz.each(sent_piece))

    @pl.when(z < N_COL)
    def _():
        spot = lax.rem(z, N_COL)
        hz_in[pl.ds(z, 1)] = hz_out[pl.ds(spot, 1)]
        reduce_hz.wait_recv(lambda i: hz_in.at[i])
        hz_all[pl.ds(spot, 1)] = jnp.sum(hz_in[...].astype(F32), axis=0).astype(BF)[None]
        gather_hz.start(lambda i: hz_all.at[spot], lambda i: hz_all.at[lax.rem(i, N_COL)])

    def sent_sum():
        @pl.when(z < N_COL)
        def _():
            gather_hz.each(
                lambda k: gather_hz.copy(
                    k, lambda i: hz_all.at[0], lambda i: hz_all.at[lax.rem(i, N_COL)]
                ).wait_send()
            )

    sends.append(sent_sum)
    gather_h = []
    for h in range(2):

        def take_piece(k, h=h):
            @pl.when(lax.div(lax.rem(z + NZ - k, NZ), HALF_COL) == h)
            def _():
                gather_hz.arrival(k, lambda i: hz_all.at[lax.rem(i, N_COL)]).wait_recv()

        gather_hz.each(take_piece)
        part = pl.ds(h * HALF_COL, HALF_COL)
        h_all[pl.ds(y, 1), part] = hz_all[part][None]
        gather_h.append(y_axis(6 + h))
        sends.append(
            gather_h[h].start(
                lambda i, part=part: hz_all.at[part], lambda i, part=part: h_all.at[i, part]
            )
        )
    for h in range(2):
        gather_h[h].wait_recv(lambda i: h_all.at[i, pl.ds(h * HALF_COL, HALF_COL)])
        for r in range(NY):
            for c in range(h * HALF_COL, (h + 1) * HALF_COL):
                rows = slice(r * ROW_PIECE, (r + 1) * ROW_PIECE)
                head_ref[rows, c * 128 : (c + 1) * 128] = h_all[r, c].astype(F32)

    for wait in sends:
        wait()


def place(q_ref, p_ref, h_ref, q_out, p_out, h_out, sem):
    copies = [
        pltpu.make_async_copy(src, dst, sem.at[i])
        for i, (src, dst) in enumerate(((h_ref, h_out), (q_ref, q_out), (p_ref, p_out)))
    ]
    for copy in copies:
        copy.start()
    for copy in copies:
        copy.wait()


def shards(
    query_states, passage_states, head_weight, candidates, counts, teacher_scores, owner_map
):
    vmem = pltpu.VMEM
    scratch = [
        vmem((NY, ROWS, D), BF),
        vmem((NZ, 16, HALF), BF),
        vmem((NG, 16, HALF), BF),
        vmem((NY, ROWS, PB), F32),
        vmem((NY, 8, QB), F32),
        vmem((NZ, 16, HALF), BF),
        vmem((NY, ROWS, D), BF),
        vmem((NG, 16, HALF), BF),
        vmem((NY, 2, ROW_PIECE, HALF), BF),
        vmem((NZ, ROW_PIECE, 128), BF),
        vmem((N_COL, ROW_PIECE, 128), BF),
        vmem((NY, N_COL, ROW_PIECE, 128), BF),
        vmem((OWN, D), BF),
        vmem((1, 16, HALF), BF),
        vmem((D, D), BF),
        vmem((ROWS, CAND), jnp.int32),
        pltpu.SMEM((ROWS,), jnp.int32),
        vmem((ROWS, CAND), F32),
        vmem((1, POOL), jnp.int32),
        vmem((ROWS, CAND), jnp.int32),
        vmem((ROWS, CAND), jnp.int32),
        vmem((4, ROWS, CAND), F32),
        vmem((ROWS * NY, PB), F32),
        vmem((NY, ROWS, PB), F32),
        vmem((8, QB), F32),
        vmem((NZ, 16, HALF), BF),
        vmem((NY, ROWS, D), BF),
        vmem((NY, 2, ROW_PIECE, HALF), BF),
        vmem((N_COL, ROW_PIECE, 128), BF),
        vmem((NY, ROWS, D), BF),
        vmem((PB, D), BF),
        vmem((PB, D), BF),
        vmem((NG * OWN, D), BF),
        vmem((NG * OWN, D), F32),
        vmem((NG * OWN, D), F32),
        vmem((NG * OWN, D), F32),
        pltpu.SemaphoreType.DMA((7,)),
        pltpu.SemaphoreType.DMA((8, NY - 1)),
        pltpu.SemaphoreType.DMA((8, NY - 1)),
        pltpu.SemaphoreType.DMA((4, NZ - 1)),
        pltpu.SemaphoreType.DMA((4, NZ - 1)),
        pltpu.SemaphoreType.DMA((2, NG - 1)),
        pltpu.SemaphoreType.DMA((2, NG - 1)),
    ]
    outs = (((ROWS, D), BF), ((OWN, D), BF), ((OUT_ROWS, D), F32))
    results = pl.pallas_call(
        kernel,
        out_shape=tuple(vmem(shape, dtype) for shape, dtype in outs),
        in_specs=[pl.BlockSpec(memory_space=pl.ANY)] * 7,
        out_specs=tuple([pl.BlockSpec(memory_space=vmem)] * 3),
        scratch_shapes=scratch,
        name="distill",
        compiler_params=pltpu.CompilerParams(
            collective_id=0, has_side_effects=True, vmem_limit_bytes=61 * 1024 * 1024
        ),
    )(query_states, passage_states, head_weight, candidates, counts, teacher_scores, owner_map)
    return pl.pallas_call(
        place,
        out_shape=tuple(jax.ShapeDtypeStruct(shape, dtype) for shape, dtype in outs),
        in_specs=[pl.BlockSpec(memory_space=pl.ANY)] * 3,
        out_specs=tuple([pl.BlockSpec(memory_space=pl.ANY)] * 3),
        scratch_shapes=[pltpu.SemaphoreType.DMA((3,))],
        name="place",
    )(*(pltpu.with_memory_space_constraint(result, vmem) for result in results))


def solution(mesh):
    rows = P(("grp", "dev"), None)
    in_specs = (rows, rows, P(), rows, P(("grp", "dev")), rows, P("grp", None))
    out_specs = (rows, rows, P("grp", None))
    return jax.shard_map(shards, mesh=mesh, in_specs=in_specs, out_specs=out_specs, check_vma=False)
```

```python
import functools

import jax
import jax.numpy as jnp
from jax import lax
from jax.experimental import pallas as pl
from jax.experimental.pallas import tpu as pltpu
from jax.sharding import PartitionSpec as P

MESH = pl.DeviceIdType.MESH
NG, NZ, NY = 8, 12, 8
ROWS, OWN, D, CAND, POOL = 32, 8, 1024, 256, 768
QB = NY * ROWS
PB = 128
HALF = D // 2
OUT_ROWS = D // NG
ROW_PIECE = OUT_ROWS // NY
N_COL = D // 128
HALF_COL = N_COL // 2
BF, F32 = jnp.bfloat16, jnp.float32
FAR = -1.0e30
Q_ORDER = (0, 2, 6, 1, 7, 3, 5, 4)


def dot(a, b, ca, cb):
    return lax.dot_general(a, b, (((ca,), (cb,)), ((), ())), preferred_element_type=F32)


def fold(rows):
    return jnp.concatenate([rows[:, :, :HALF], rows[:, :, HALF:]], axis=1).astype(BF)


def unfold(block):
    wide = block.astype(F32)
    wide = jnp.concatenate([wide[:, :OWN, :], wide[:, OWN:, :]], axis=2)
    return wide.reshape(wide.shape[0] * OWN, D)


def far_first(n):
    return sorted(range(1, n), key=lambda k: -min(k, n - k))


class Exchange:
    def __init__(self, n, me, device, send_sem, recv_sem):
        self.n, self.me, self.device = n, me, device
        self.send_sem, self.recv_sem = send_sem, recv_sem

    def copy(self, k, src, dst):
        peer = lax.rem(self.me + k, self.n)
        return pltpu.make_async_remote_copy(
            src_ref=src(peer),
            dst_ref=dst(self.me),
            send_sem=self.send_sem.at[k - 1],
            recv_sem=self.recv_sem.at[k - 1],
            device_id=self.device(peer),
            device_id_type=MESH,
        )

    def arrival(self, k, dst):
        sender = lax.rem(self.me + self.n - k, self.n)
        return pltpu.make_async_remote_copy(
            src_ref=dst(sender),
            dst_ref=dst(sender),
            send_sem=self.send_sem.at[k - 1],
            recv_sem=self.recv_sem.at[k - 1],
            device_id=self.device(sender),
            device_id_type=MESH,
        )

    def each(self, body):
        def step(k, carry):
            body(k)
            return carry

        lax.fori_loop(1, self.n, step, 0)

    def far_first(self, body):
        for k in far_first(self.n):
            body(k)

    def start(self, src, dst):
        self.far_first(lambda k: self.copy(k, src, dst).start())
        return lambda: self.each(lambda k: self.copy(k, src, dst).wait_send())

    def wait_recv(self, dst):
        self.each(lambda k: self.arrival(k, dst).wait_recv())


def kernel(
    qs_hbm, ps_hbm, w_hbm, cand_hbm, counts_hbm, teach_hbm, own_hbm,
    qgrad_ref, pgrad_ref, head_ref,
    qs_all, ps_all, pg_all, t_all, st_all, v_in, u_in, vg_all, h_in, hz_in, hz_all, h_all,
    ps_loc, ps_mine, w_ref, cand_ref, counts_ref, teach_ref, own_ref,
    b_ref, y_ref, parts_ref, tb_ref, t_out, st_out, v_out, u_out, h_out, hz_out,
    q_ref, p128_ref, ps128_ref, p64_ref, ps64_ref, v64_ref, vw_ref,
    local_sem, ysend, yrecv, zsend, zrecv, gsend, grecv,
):
    g = lax.axis_index("grp")
    d = lax.axis_index("dev")
    z, y = d // NY, lax.rem(d, NY)
    scale = D ** -0.5

    def on_y(i):
        return (g, z * NY + i)

    def on_z(i):
        return (g, i * NY + y)

    def on_g(i):
        return (i, d)

    def y_axis(s):
        return Exchange(NY, y, on_y, ysend.at[s], yrecv.at[s])

    def z_axis(s):
        return Exchange(NZ, z, on_z, zsend.at[s], zrecv.at[s])

    def g_axis(s):
        return Exchange(NG, g, on_g, gsend.at[s], grecv.at[s])

    sends = []

    barrier = pltpu.get_barrier_semaphore()
    for n, me, device in ((NZ, z, on_z), (NY, y, on_y), (NG, g, on_g)):
        for k in far_first(n):
            pl.semaphore_signal(
                barrier, inc=1, device_id=device(lax.rem(me + k, n)), device_id_type=MESH
            )

    locals_ = [
        pltpu.make_async_copy(src, dst, local_sem.at[i])
        for i, (src, dst) in enumerate(
            [
                (ps_hbm, ps_loc),
                (qs_hbm, qs_all.at[y]),
                (cand_hbm, cand_ref),
                (own_hbm, own_ref),
                (counts_hbm, counts_ref),
                (teach_hbm, teach_ref),
                (w_hbm, w_ref),
            ]
        )
    ]
    for copy in locals_:
        copy.start()
    locals_[0].wait()
    mine = fold(ps_loc[...].astype(F32)[None])
    ps_mine[...] = mine
    ps_all[pl.ds(z, 1)] = mine
    pg_all[pl.ds(g, 1)] = mine
    locals_[1].wait()

    pl.semaphore_wait(barrier, NZ + NY + NG - 3)
    gather_q, gather_p, gather_pg = y_axis(0), z_axis(0), g_axis(0)
    for k in (2, 6, 1, 7):
        copy = gather_q.copy(k, lambda i: qs_all.at[y], lambda i: qs_all.at[i])
        copy.start()
        sends.append(copy.wait_send)
    sends.append(gather_p.start(lambda i: ps_mine.at[0], lambda i: ps_all.at[i]))
    sends.append(gather_pg.start(lambda i: ps_mine.at[0], lambda i: pg_all.at[i]))

    for copy in locals_[2:6]:
        copy.wait()
    row_id = lax.broadcasted_iota(jnp.int32, (ROWS, 128), 0)
    lane_id = lax.broadcasted_iota(jnp.int32, (ROWS, 128), 1)
    limit = jnp.zeros((ROWS, 128), jnp.int32)
    for i in range(ROWS):
        limit = jnp.where(row_id == i, counts_ref[i], limit)
    storage = []
    for c in range(CAND // 128):
        ids = cand_ref[:, c * 128 : (c + 1) * 128]
        low, high = ids & 127, ids >> 7
        row = jnp.zeros((ROWS, 128), jnp.int32)
        for t in range(POOL // 128):
            table = jnp.broadcast_to(own_ref[:, t * 128 : (t + 1) * 128], (ROWS, 128))
            picked = jnp.take_along_axis(table, low, axis=1, mode="promise_in_bounds")
            row = jnp.where(high == t, picked, row)
        storage.append(row)
    storage = jnp.concatenate(storage, axis=1)
    b_ref[...] = ((storage >> 6) << 3) | (storage & 7)
    y_ref[...] = (storage >> 3) & 7
    slot_id = jnp.concatenate([lane_id, lane_id + 128], axis=1)
    valid = slot_id < jnp.concatenate([limit, limit], axis=1)
    values = teach_ref[...]
    top = jnp.max(jnp.where(valid, values, -jnp.inf), axis=1, keepdims=True)
    weights = jnp.where(valid, jnp.exp(jnp.where(valid, values - top, 0.0)), 0.0)
    teacher = weights / jnp.sum(weights, axis=1, keepdims=True)
    part = teacher.astype(BF).astype(F32)
    parts_ref[0] = part
    rest = teacher - part
    part = rest.astype(BF).astype(F32)
    parts_ref[1] = part
    parts_ref[2] = rest - part
    parts_ref[3] = jnp.where(valid, 1.0, 0.0)

    block_id = lax.broadcasted_iota(jnp.int32, (PB, CAND), 0)
    owner_id = lax.broadcasted_iota(jnp.int32, (NY, CAND), 0)

    def densify(i, carry):
        hot = jnp.where(block_id == b_ref[pl.ds(i, 1), :], 1.0, 0.0).astype(BF)
        mask = owner_id == y_ref[pl.ds(i, 1), :]
        lhs = jnp.concatenate(
            [jnp.where(mask, parts_ref[n, pl.ds(i, 1), :], 0.0) for n in range(4)], axis=0
        ).astype(BF)
        out = dot(lhs, hot, 1, 1)
        dense = out[0:8] + (out[8:16] + out[16:24])
        tb_ref[pl.ds(pl.multiple_of(i * NY, NY), NY), :] = jnp.where(out[24:32] > 0.5, dense, -1.0)
        return carry

    lax.fori_loop(0, ROWS, densify, 0, unroll=4)
    for k, shift, s, n in ((2, 1, 0, 2), (6, -1, 0, 4), (2, 2, 0, 3), (6, -2, 8, 0)):
        if abs(shift) == 1:
            gather_q.arrival(k, lambda i: qs_all.at[i]).wait_recv()
        block = qs_all.at[lax.rem(y + NY - k, NY)]
        if abs(shift) == 2:
            block = block.at[pl.ds(ROWS // 2 * (shift < 0), ROWS // 2)]
        copy = pltpu.make_async_remote_copy(
            src_ref=block,
            dst_ref=block,
            send_sem=ysend.at[s, n],
            recv_sem=yrecv.at[s, n],
            device_id=on_y(lax.rem(y + shift + NY, NY)),
            device_id_type=MESH,
        )
        copy.start()
        sends.append(copy.wait_send)

    for i in range(NY):
        t_out[i] = tb_ref[pl.ds(i, ROWS, stride=NY), :]
    t_all[pl.ds(y, 1)] = t_out[pl.ds(y, 1)]
    gather_t = y_axis(1)
    sends.append(gather_t.start(lambda i: t_out.at[i], lambda i: t_all.at[i]))


    locals_[6].wait()
    gather_p.wait_recv(lambda i: ps_all.at[i])
    gather_pg.wait_recv(lambda i: pg_all.at[i])
    ps128_ref[...] = jnp.concatenate(
        [unfold(ps_all[...]), jnp.zeros((PB - NZ * OWN, D), F32)], axis=0
    ).astype(BF)
    ps64_ref[...] = unfold(pg_all[...])
    p128_ref[...] = dot(ps128_ref[...], w_ref[...], 1, 0).astype(BF)
    p64_ref[...] = dot(ps64_ref[...].astype(BF), w_ref[...], 1, 0).astype(BF)
    for part in (Q_ORDER[:5], Q_ORDER[5:]):
        spots = []
        for k in part:
            if k in (1, 7, 3, 5):
                gather_q.arrival(k, lambda i: qs_all.at[i]).wait_recv()
            spots.append(lax.rem(y + NY - k, NY))
            if k == 4:
                for s, n, start in ((0, 3, 0), (8, 0, ROWS // 2)):
                    block = qs_all.at[spots[-1], pl.ds(start, ROWS // 2)]
                    pltpu.make_async_copy(block, block, yrecv.at[s, n]).wait()
        some = jnp.concatenate([qs_all[pl.ds(i, 1)] for i in spots], axis=0)
        done = dot(some.reshape(len(spots) * ROWS, D), w_ref[...], 1, 0).astype(BF)
        for n, i in enumerate(spots):
            q_ref[pl.ds(i, 1)] = done[n * ROWS : (n + 1) * ROWS][None]
    qs_block = qs_all[...].reshape(QB, D)


    score = scale * dot(p128_ref[...], q_ref[...].reshape(QB, D), 1, 1)
    gather_t.wait_recv(lambda i: t_all.at[i])
    teach = t_all[...].reshape(QB, PB).T
    used = teach >= 0.0
    local_top = jnp.max(jnp.where(used, score, FAR), axis=0, keepdims=True)
    expo = jnp.where(used, jnp.exp(jnp.where(used, score - local_top, 0.0)), 0.0)
    local_sum = jnp.sum(expo, axis=0, keepdims=True)
    stats = jnp.where(
        lax.broadcasted_iota(jnp.int32, (2, QB), 0) == 0, local_top, local_sum
    )
    st_out[...] = stats
    st_all[pl.ds(y, 1)] = stats[None]
    stats_x = y_axis(2)
    sends.append(stats_x.start(lambda i: st_out, lambda i: st_all.at[i]))
    stats_x.wait_recv(lambda i: st_all.at[i])
    tops = st_all[:, 0:1, :]
    top = jnp.max(tops, axis=0)
    total = jnp.sum(st_all[:, 1:2, :] * jnp.exp(tops - top[None]), axis=0)
    student = expo * (jnp.exp(local_top - top) / total)
    dscore = jnp.where(used, 256.0 * (student - teach), 0.0).astype(BF)


    v_part = scale * dot(dscore, qs_block, 1, 0)
    v_out[...] = fold(v_part[: NZ * OWN].reshape(NZ, OWN, D))
    v_in[pl.ds(z, 1)] = v_out[pl.ds(z, 1)]
    reduce_v = z_axis(1)
    sends.append(reduce_v.start(lambda i: v_out.at[i], lambda i: v_in.at[i]))
    u_part = scale * dot(dscore.astype(F32).T.astype(BF), ps128_ref[...], 1, 0)
    u_out[...] = u_part.astype(BF).reshape(NY, ROWS, D)
    u_in[pl.ds(y, 1)] = u_out[pl.ds(y, 1)]
    reduce_u = y_axis(3)
    sends.append(reduce_u.start(lambda i: u_out.at[i], lambda i: u_in.at[i]))


    reduce_v.wait_recv(lambda i: v_in.at[i])
    v_sum = jnp.sum(v_in[...].astype(F32), axis=0)
    vg_all[pl.ds(g, 1)] = v_sum.astype(BF)[None]
    gather_v = g_axis(1)
    sends.append(gather_v.start(lambda i: vg_all.at[g], lambda i: vg_all.at[i]))
    gather_v.wait_recv(lambda i: vg_all.at[i])
    v64_ref[...] = unfold(vg_all[...])
    cols = pl.ds(pl.multiple_of(g * OUT_ROWS, OUT_ROWS), OUT_ROWS)
    left = jnp.concatenate([v64_ref[:, cols], ps64_ref[:, cols]], axis=0).T.astype(BF)
    v64 = v64_ref[...].astype(BF)
    reduce_h = []
    for h in range(2):
        half = slice(h * HALF, (h + 1) * HALF)
        vw = dot(v64, w_ref[:, half], 1, 0).astype(BF)
        vw_ref[:, half] = vw.astype(F32)
        right = jnp.concatenate([p64_ref[:, half], vw], axis=0)
        h_out[:, h] = dot(left, right, 1, 0).astype(BF).reshape(NY, ROW_PIECE, HALF)
        h_in[pl.ds(y, 1), h] = h_out[pl.ds(y, 1), h]
        reduce_h.append(y_axis(4 + h))
        sends.append(
            reduce_h[h].start(lambda i, h=h: h_out.at[i, h], lambda i, h=h: h_in.at[i, h])
        )

    reduce_u.wait_recv(lambda i: u_in.at[i])
    u_sum = jnp.sum(u_in[...].astype(F32), axis=0).astype(BF)
    gq = dot(u_sum, w_ref[...], 1, 0)
    gp = vw_ref[pl.ds(pl.multiple_of(g * OWN, OWN), OWN), :]
    rows = jnp.concatenate([gq, gp, gp], axis=0).astype(BF)
    grads = dot(rows, w_ref[...], 1, 1)
    qgrad_ref[...] = grads[:ROWS].astype(BF)
    pgrad_ref[...] = grads[ROWS : ROWS + OWN].astype(BF)


    reduce_hz, gather_hz = z_axis(2), z_axis(3)
    for h in range(2):
        reduce_h[h].wait_recv(lambda i: h_in.at[i, h])
        h_sum = jnp.sum(h_in[:, h].astype(F32), axis=0).astype(BF)
        for i in range(HALF_COL):
            hz_out[h * HALF_COL + i] = h_sum[:, i * 128 : (i + 1) * 128]

        def owner(k, h=h):
            return lax.div(lax.rem(z + k, NZ), HALF_COL) == h

        def piece(k):
            return reduce_hz.copy(
                k, lambda i: hz_out.at[lax.rem(i, N_COL)], lambda i: hz_in.at[i]
            )

        def send_piece(k, owner=owner):
            @pl.when(owner(k))
            def _():
                piece(k).start()

        def sent_piece(k, owner=owner):
            @pl.when(owner(k))
            def _():
                piece(k).wait_send()

        reduce_hz.far_first(send_piece)
        sends.append(lambda sent_piece=sent_piece: reduce_hz.each(sent_piece))

    @pl.when(z < N_COL)
    def _():
        spot = lax.rem(z, N_COL)
        hz_in[pl.ds(z, 1)] = hz_out[pl.ds(spot, 1)]
        reduce_hz.wait_recv(lambda i: hz_in.at[i])
        hz_all[pl.ds(spot, 1)] = jnp.sum(hz_in[...].astype(F32), axis=0).astype(BF)[None]
        gather_hz.start(lambda i: hz_all.at[spot], lambda i: hz_all.at[lax.rem(i, N_COL)])

    def sent_sum():
        @pl.when(z < N_COL)
        def _():
            gather_hz.each(
                lambda k: gather_hz.copy(
                    k, lambda i: hz_all.at[0], lambda i: hz_all.at[lax.rem(i, N_COL)]
                ).wait_send()
            )

    sends.append(sent_sum)
    gather_h = []
    for h in range(2):

        def take_piece(k, h=h):
            @pl.when(lax.div(lax.rem(z + NZ - k, NZ), HALF_COL) == h)
            def _():
                gather_hz.arrival(k, lambda i: hz_all.at[lax.rem(i, N_COL)]).wait_recv()

        gather_hz.each(take_piece)
        part = pl.ds(h * HALF_COL, HALF_COL)
        h_all[pl.ds(y, 1), part] = hz_all[part][None]
        gather_h.append(y_axis(6 + h))
        sends.append(
            gather_h[h].start(
                lambda i, part=part: hz_all.at[part], lambda i, part=part: h_all.at[i, part]
            )
        )
    for h in range(2):
        gather_h[h].wait_recv(lambda i: h_all.at[i, pl.ds(h * HALF_COL, HALF_COL)])
        for r in range(NY):
            for c in range(h * HALF_COL, (h + 1) * HALF_COL):
                rows = slice(r * ROW_PIECE, (r + 1) * ROW_PIECE)
                head_ref[rows, c * 128 : (c + 1) * 128] = h_all[r, c].astype(F32)

    for wait in sends:
        wait()


def place(q_ref, p_ref, h_ref, q_out, p_out, h_out, sem):
    copies = [
        pltpu.make_async_copy(src, dst, sem.at[i])
        for i, (src, dst) in enumerate(((h_ref, h_out), (q_ref, q_out), (p_ref, p_out)))
    ]
    for copy in copies:
        copy.start()
    for copy in copies:
        copy.wait()


def shards(
    query_states, passage_states, head_weight, candidates, counts, teacher_scores, owner_map
):
    vmem = pltpu.VMEM
    scratch = [
        vmem((NY, ROWS, D), BF),
        vmem((NZ, 16, HALF), BF),
        vmem((NG, 16, HALF), BF),
        vmem((NY, ROWS, PB), F32),
        vmem((NY, 2, QB), F32),
        vmem((NZ, 16, HALF), BF),
        vmem((NY, ROWS, D), BF),
        vmem((NG, 16, HALF), BF),
        vmem((NY, 2, ROW_PIECE, HALF), BF),
        vmem((NZ, ROW_PIECE, 128), BF),
        vmem((N_COL, ROW_PIECE, 128), BF),
        vmem((NY, N_COL, ROW_PIECE, 128), BF),
        vmem((OWN, D), BF),
        vmem((1, 16, HALF), BF),
        vmem((D, D), BF),
        vmem((ROWS, CAND), jnp.int32),
        pltpu.SMEM((ROWS,), jnp.int32),
        vmem((ROWS, CAND), F32),
        vmem((1, POOL), jnp.int32),
        vmem((ROWS, CAND), jnp.int32),
        vmem((ROWS, CAND), jnp.int32),
        vmem((4, ROWS, CAND), F32),
        vmem((ROWS * NY, PB), F32),
        vmem((NY, ROWS, PB), F32),
        vmem((2, QB), F32),
        vmem((NZ, 16, HALF), BF),
        vmem((NY, ROWS, D), BF),
        vmem((NY, 2, ROW_PIECE, HALF), BF),
        vmem((N_COL, ROW_PIECE, 128), BF),
        vmem((NY, ROWS, D), BF),
        vmem((PB, D), BF),
        vmem((PB, D), BF),
        vmem((NG * OWN, D), BF),
        vmem((NG * OWN, D), F32),
        vmem((NG * OWN, D), F32),
        vmem((NG * OWN, D), F32),
        pltpu.SemaphoreType.DMA((7,)),
        pltpu.SemaphoreType.DMA((9, NY - 1)),
        pltpu.SemaphoreType.DMA((9, NY - 1)),
        pltpu.SemaphoreType.DMA((4, NZ - 1)),
        pltpu.SemaphoreType.DMA((4, NZ - 1)),
        pltpu.SemaphoreType.DMA((2, NG - 1)),
        pltpu.SemaphoreType.DMA((2, NG - 1)),
    ]
    outs = (((ROWS, D), BF), ((OWN, D), BF), ((OUT_ROWS, D), F32))
    results = pl.pallas_call(
        kernel,
        out_shape=tuple(vmem(shape, dtype) for shape, dtype in outs),
        in_specs=[pl.BlockSpec(memory_space=pl.ANY)] * 7,
        out_specs=tuple([pl.BlockSpec(memory_space=vmem)] * 3),
        scratch_shapes=scratch,
        name="distill",
        compiler_params=pltpu.CompilerParams(
            collective_id=0, has_side_effects=True, vmem_limit_bytes=61 * 1024 * 1024
        ),
    )(query_states, passage_states, head_weight, candidates, counts, teacher_scores, owner_map)
    return pl.pallas_call(
        place,
        out_shape=tuple(jax.ShapeDtypeStruct(shape, dtype) for shape, dtype in outs),
        in_specs=[pl.BlockSpec(memory_space=pl.ANY)] * 3,
        out_specs=tuple([pl.BlockSpec(memory_space=pl.ANY)] * 3),
        scratch_shapes=[pltpu.SemaphoreType.DMA((3,))],
        name="place",
    )(*(pltpu.with_memory_space_constraint(result, vmem) for result in results))


def solution(mesh):
    rows = P(("grp", "dev"), None)
    in_specs = (rows, rows, P(), rows, P(("grp", "dev")), rows, P("grp", None))
    out_specs = (rows, rows, P("grp", None))
    return jax.shard_map(shards, mesh=mesh, in_specs=in_specs, out_specs=out_specs, check_vma=False)
```

```python
import functools

import jax
import jax.numpy as jnp
from jax import lax
from jax.experimental import pallas as pl
from jax.experimental.pallas import tpu as pltpu
from jax.sharding import PartitionSpec as P

MESH = pl.DeviceIdType.MESH
NG, NZ, NY = 8, 12, 8
ROWS, OWN, D, CAND, POOL = 32, 8, 1024, 256, 768
QB = NY * ROWS
PB = 128
HALF = D // 2
OUT_ROWS = D // NG
ROW_PIECE = OUT_ROWS // NY
N_COL = D // 128
HALF_COL = N_COL // 2
BF, F32 = jnp.bfloat16, jnp.float32
FAR = -1.0e30
Q_ORDER = (0, 2, 6, 1, 7, 3, 5, 4)


def dot(a, b, ca, cb):
    return lax.dot_general(a, b, (((ca,), (cb,)), ((), ())), preferred_element_type=F32)


def fold(rows):
    return jnp.concatenate([rows[:, :, :HALF], rows[:, :, HALF:]], axis=1).astype(BF)


def unfold(block):
    wide = block.astype(F32)
    wide = jnp.concatenate([wide[:, :OWN, :], wide[:, OWN:, :]], axis=2)
    return wide.reshape(wide.shape[0] * OWN, D)


def far_first(n):
    return sorted(range(1, n), key=lambda k: -min(k, n - k))


class Exchange:
    def __init__(self, n, me, device, send_sem, recv_sem):
        self.n, self.me, self.device = n, me, device
        self.send_sem, self.recv_sem = send_sem, recv_sem

    def copy(self, k, src, dst):
        peer = lax.rem(self.me + k, self.n)
        return pltpu.make_async_remote_copy(
            src_ref=src(peer),
            dst_ref=dst(self.me),
            send_sem=self.send_sem.at[k - 1],
            recv_sem=self.recv_sem.at[k - 1],
            device_id=self.device(peer),
            device_id_type=MESH,
        )

    def arrival(self, k, dst):
        sender = lax.rem(self.me + self.n - k, self.n)
        return pltpu.make_async_remote_copy(
            src_ref=dst(sender),
            dst_ref=dst(sender),
            send_sem=self.send_sem.at[k - 1],
            recv_sem=self.recv_sem.at[k - 1],
            device_id=self.device(sender),
            device_id_type=MESH,
        )

    def each(self, body):
        def step(k, carry):
            body(k)
            return carry

        lax.fori_loop(1, self.n, step, 0)

    def far_first(self, body):
        for k in far_first(self.n):
            body(k)

    def start(self, src, dst):
        self.far_first(lambda k: self.copy(k, src, dst).start())
        return lambda: self.each(lambda k: self.copy(k, src, dst).wait_send())

    def wait_recv(self, dst):
        self.each(lambda k: self.arrival(k, dst).wait_recv())


def kernel(
    qs_hbm, ps_hbm, w_hbm, cand_hbm, counts_hbm, teach_hbm, own_hbm,
    qgrad_ref, pgrad_ref, head_ref,
    qs_all, ps_all, pg_all, t_all, st_all, v_in, u_in, vg_all, h_in, hz_in, hz_all, h_all,
    ps_loc, ps_mine, w_ref, cand_ref, counts_ref, teach_ref, own_ref,
    b_ref, y_ref, parts_ref, tb_ref, t_out, st_out, v_out, u_out, h_out, hz_out,
    q_ref, p128_ref, ps128_ref, p64_ref, ps64_ref, v64_ref, vw_ref,
    local_sem, ysend, yrecv, zsend, zrecv, gsend, grecv,
):
    g = lax.axis_index("grp")
    d = lax.axis_index("dev")
    z, y = d // NY, lax.rem(d, NY)
    scale = D ** -0.5

    def on_y(i):
        return (g, z * NY + i)

    def on_z(i):
        return (g, i * NY + y)

    def on_g(i):
        return (i, d)

    def y_axis(s):
        return Exchange(NY, y, on_y, ysend.at[s], yrecv.at[s])

    def z_axis(s):
        return Exchange(NZ, z, on_z, zsend.at[s], zrecv.at[s])

    def g_axis(s):
        return Exchange(NG, g, on_g, gsend.at[s], grecv.at[s])

    sends = []

    barrier = pltpu.get_barrier_semaphore()
    for n, me, device in ((NZ, z, on_z), (NY, y, on_y), (NG, g, on_g)):
        for k in far_first(n):
            pl.semaphore_signal(
                barrier, inc=1, device_id=device(lax.rem(me + k, n)), device_id_type=MESH
            )

    locals_ = [
        pltpu.make_async_copy(src, dst, local_sem.at[i])
        for i, (src, dst) in enumerate(
            [
                (ps_hbm, ps_loc),
                (qs_hbm, qs_all.at[y]),
                (cand_hbm, cand_ref),
                (own_hbm, own_ref),
                (counts_hbm, counts_ref),
                (teach_hbm, teach_ref),
                (w_hbm, w_ref),
            ]
        )
    ]
    for copy in locals_:
        copy.start()
    locals_[0].wait()
    mine = fold(ps_loc[...].astype(F32)[None])
    ps_mine[...] = mine
    ps_all[pl.ds(z, 1)] = mine
    pg_all[pl.ds(g, 1)] = mine
    locals_[1].wait()

    for copy in locals_[2:6]:
        copy.wait()
    row_id = lax.broadcasted_iota(jnp.int32, (ROWS, 128), 0)
    lane_id = lax.broadcasted_iota(jnp.int32, (ROWS, 128), 1)
    limit = jnp.zeros((ROWS, 128), jnp.int32)
    for i in range(ROWS):
        limit = jnp.where(row_id == i, counts_ref[i], limit)
    storage = []
    for c in range(CAND // 128):
        ids = cand_ref[:, c * 128 : (c + 1) * 128]
        low, high = ids & 127, ids >> 7
        row = jnp.zeros((ROWS, 128), jnp.int32)
        for t in range(POOL // 128):
            table = jnp.broadcast_to(own_ref[:, t * 128 : (t + 1) * 128], (ROWS, 128))
            picked = jnp.take_along_axis(table, low, axis=1, mode="promise_in_bounds")
            row = jnp.where(high == t, picked, row)
        storage.append(row)
    storage = jnp.concatenate(storage, axis=1)
    b_ref[...] = ((storage >> 6) << 3) | (storage & 7)
    y_ref[...] = (storage >> 3) & 7
    slot_id = jnp.concatenate([lane_id, lane_id + 128], axis=1)
    valid = slot_id < jnp.concatenate([limit, limit], axis=1)
    values = teach_ref[...]
    top = jnp.max(jnp.where(valid, values, -jnp.inf), axis=1, keepdims=True)
    weights = jnp.where(valid, jnp.exp(jnp.where(valid, values - top, 0.0)), 0.0)
    teacher = weights / jnp.sum(weights, axis=1, keepdims=True)
    part = teacher.astype(BF).astype(F32)
    parts_ref[0] = part
    rest = teacher - part
    part = rest.astype(BF).astype(F32)
    parts_ref[1] = part
    parts_ref[2] = rest - part
    parts_ref[3] = jnp.where(valid, 1.0, 0.0)

    pl.semaphore_wait(barrier, NZ + NY + NG - 3)
    gather_q, gather_p, gather_pg = y_axis(0), z_axis(0), g_axis(0)
    for k in (2, 6, 1, 7):
        copy = gather_q.copy(k, lambda i: qs_all.at[y], lambda i: qs_all.at[i])
        copy.start()
        sends.append(copy.wait_send)
    sends.append(gather_p.start(lambda i: ps_mine.at[0], lambda i: ps_all.at[i]))
    sends.append(gather_pg.start(lambda i: ps_mine.at[0], lambda i: pg_all.at[i]))
    block_id = lax.broadcasted_iota(jnp.int32, (PB, CAND), 0)
    owner_id = lax.broadcasted_iota(jnp.int32, (NY, CAND), 0)

    def densify(i, carry):
        hot = jnp.where(block_id == b_ref[pl.ds(i, 1), :], 1.0, 0.0).astype(BF)
        mask = owner_id == y_ref[pl.ds(i, 1), :]
        lhs = jnp.concatenate(
            [jnp.where(mask, parts_ref[n, pl.ds(i, 1), :], 0.0) for n in range(4)], axis=0
        ).astype(BF)
        out = dot(lhs, hot, 1, 1)
        dense = out[0:8] + (out[8:16] + out[16:24])
        tb_ref[pl.ds(pl.multiple_of(i * NY, NY), NY), :] = jnp.where(out[24:32] > 0.5, dense, -1.0)
        return carry

    lax.fori_loop(0, ROWS, densify, 0, unroll=4)
    for k, shift, s, n in ((2, 1, 0, 2), (6, -1, 0, 4), (2, 2, 0, 3), (6, -2, 8, 0)):
        if abs(shift) == 1:
            gather_q.arrival(k, lambda i: qs_all.at[i]).wait_recv()
        block = qs_all.at[lax.rem(y + NY - k, NY)]
        if abs(shift) == 2:
            block = block.at[pl.ds(ROWS // 2 * (shift < 0), ROWS // 2)]
        copy = pltpu.make_async_remote_copy(
            src_ref=block,
            dst_ref=block,
            send_sem=ysend.at[s, n],
            recv_sem=yrecv.at[s, n],
            device_id=on_y(lax.rem(y + shift + NY, NY)),
            device_id_type=MESH,
        )
        copy.start()
        sends.append(copy.wait_send)

    for i in range(NY):
        t_out[i] = tb_ref[pl.ds(i, ROWS, stride=NY), :]
    t_all[pl.ds(y, 1)] = t_out[pl.ds(y, 1)]
    gather_t = y_axis(1)
    sends.append(gather_t.start(lambda i: t_out.at[i], lambda i: t_all.at[i]))


    locals_[6].wait()
    gather_p.wait_recv(lambda i: ps_all.at[i])
    ps128_ref[...] = jnp.concatenate(
        [unfold(ps_all[...]), jnp.zeros((PB - NZ * OWN, D), F32)], axis=0
    ).astype(BF)
    p128_ref[...] = dot(ps128_ref[...], w_ref[...], 1, 0).astype(BF)
    for part in (Q_ORDER[:5], Q_ORDER[5:]):
        spots = []
        for k in part:
            if k in (1, 7, 3, 5):
                gather_q.arrival(k, lambda i: qs_all.at[i]).wait_recv()
            spots.append(lax.rem(y + NY - k, NY))
            if k == 4:
                for s, n, start in ((0, 3, 0), (8, 0, ROWS // 2)):
                    block = qs_all.at[spots[-1], pl.ds(start, ROWS // 2)]
                    pltpu.make_async_copy(block, block, yrecv.at[s, n]).wait()
        some = jnp.concatenate([qs_all[pl.ds(i, 1)] for i in spots], axis=0)
        done = dot(some.reshape(len(spots) * ROWS, D), w_ref[...], 1, 0).astype(BF)
        for n, i in enumerate(spots):
            q_ref[pl.ds(i, 1)] = done[n * ROWS : (n + 1) * ROWS][None]
    qs_block = qs_all[...].reshape(QB, D)


    score = scale * dot(p128_ref[...], q_ref[...].reshape(QB, D), 1, 1)
    gather_t.wait_recv(lambda i: t_all.at[i])
    teach = t_all[...].reshape(QB, PB).T
    used = teach >= 0.0
    local_top = jnp.max(jnp.where(used, score, FAR), axis=0, keepdims=True)
    expo = jnp.where(used, jnp.exp(jnp.where(used, score - local_top, 0.0)), 0.0)
    local_sum = jnp.sum(expo, axis=0, keepdims=True)
    stats = jnp.where(
        lax.broadcasted_iota(jnp.int32, (2, QB), 0) == 0, local_top, local_sum
    )
    st_out[...] = stats
    st_all[pl.ds(y, 1)] = stats[None]
    stats_x = y_axis(2)
    sends.append(stats_x.start(lambda i: st_out, lambda i: st_all.at[i]))
    gather_pg.wait_recv(lambda i: pg_all.at[i])
    ps64_ref[...] = unfold(pg_all[...])
    p64_ref[...] = dot(ps64_ref[...].astype(BF), w_ref[...], 1, 0).astype(BF)
    stats_x.wait_recv(lambda i: st_all.at[i])
    tops = st_all[:, 0:1, :]
    top = jnp.max(tops, axis=0)
    total = jnp.sum(st_all[:, 1:2, :] * jnp.exp(tops - top[None]), axis=0)
    student = expo * (jnp.exp(local_top - top) / total)
    dscore = jnp.where(used, 256.0 * (student - teach), 0.0).astype(BF)


    v_part = scale * dot(dscore, qs_block, 1, 0)
    v_out[...] = fold(v_part[: NZ * OWN].reshape(NZ, OWN, D))
    v_in[pl.ds(z, 1)] = v_out[pl.ds(z, 1)]
    reduce_v = z_axis(1)
    sends.append(reduce_v.start(lambda i: v_out.at[i], lambda i: v_in.at[i]))
    u_part = scale * dot(dscore.astype(F32).T.astype(BF), ps128_ref[...], 1, 0)
    u_out[...] = u_part.astype(BF).reshape(NY, ROWS, D)
    u_in[pl.ds(y, 1)] = u_out[pl.ds(y, 1)]
    reduce_u = y_axis(3)
    sends.append(reduce_u.start(lambda i: u_out.at[i], lambda i: u_in.at[i]))


    reduce_v.wait_recv(lambda i: v_in.at[i])
    v_sum = jnp.sum(v_in[...].astype(F32), axis=0)
    vg_all[pl.ds(g, 1)] = v_sum.astype(BF)[None]
    gather_v = g_axis(1)
    sends.append(gather_v.start(lambda i: vg_all.at[g], lambda i: vg_all.at[i]))
    gather_v.wait_recv(lambda i: vg_all.at[i])
    v64_ref[...] = unfold(vg_all[...])
    cols = pl.ds(pl.multiple_of(g * OUT_ROWS, OUT_ROWS), OUT_ROWS)
    left = jnp.concatenate([v64_ref[:, cols], ps64_ref[:, cols]], axis=0).T.astype(BF)
    v64 = v64_ref[...].astype(BF)
    reduce_h = []
    for h in range(2):
        half = slice(h * HALF, (h + 1) * HALF)
        vw = dot(v64, w_ref[:, half], 1, 0).astype(BF)
        vw_ref[:, half] = vw.astype(F32)
        right = jnp.concatenate([p64_ref[:, half], vw], axis=0)
        h_out[:, h] = dot(left, right, 1, 0).astype(BF).reshape(NY, ROW_PIECE, HALF)
        h_in[pl.ds(y, 1), h] = h_out[pl.ds(y, 1), h]
        reduce_h.append(y_axis(4 + h))
        sends.append(
            reduce_h[h].start(lambda i, h=h: h_out.at[i, h], lambda i, h=h: h_in.at[i, h])
        )

    reduce_u.wait_recv(lambda i: u_in.at[i])
    u_sum = jnp.sum(u_in[...].astype(F32), axis=0).astype(BF)
    gq = dot(u_sum, w_ref[...], 1, 0)
    gp = vw_ref[pl.ds(pl.multiple_of(g * OWN, OWN), OWN), :]
    rows = jnp.concatenate([gq, gp, gp], axis=0).astype(BF)
    grads = dot(rows, w_ref[...], 1, 1)
    qgrad_ref[...] = grads[:ROWS].astype(BF)
    pgrad_ref[...] = grads[ROWS : ROWS + OWN].astype(BF)


    reduce_hz, gather_hz = z_axis(2), z_axis(3)
    for h in range(2):
        reduce_h[h].wait_recv(lambda i: h_in.at[i, h])
        h_sum = jnp.sum(h_in[:, h].astype(F32), axis=0).astype(BF)
        for i in range(HALF_COL):
            hz_out[h * HALF_COL + i] = h_sum[:, i * 128 : (i + 1) * 128]

        def owner(k, h=h):
            return lax.div(lax.rem(z + k, NZ), HALF_COL) == h

        def piece(k):
            return reduce_hz.copy(
                k, lambda i: hz_out.at[lax.rem(i, N_COL)], lambda i: hz_in.at[i]
            )

        def send_piece(k, owner=owner):
            @pl.when(owner(k))
            def _():
                piece(k).start()

        def sent_piece(k, owner=owner):
            @pl.when(owner(k))
            def _():
                piece(k).wait_send()

        reduce_hz.far_first(send_piece)
        sends.append(lambda sent_piece=sent_piece: reduce_hz.each(sent_piece))

    @pl.when(z < N_COL)
    def _():
        spot = lax.rem(z, N_COL)
        hz_in[pl.ds(z, 1)] = hz_out[pl.ds(spot, 1)]
        reduce_hz.wait_recv(lambda i: hz_in.at[i])
        hz_all[pl.ds(spot, 1)] = jnp.sum(hz_in[...].astype(F32), axis=0).astype(BF)[None]
        gather_hz.start(lambda i: hz_all.at[spot], lambda i: hz_all.at[lax.rem(i, N_COL)])

    def sent_sum():
        @pl.when(z < N_COL)
        def _():
            gather_hz.each(
                lambda k: gather_hz.copy(
                    k, lambda i: hz_all.at[0], lambda i: hz_all.at[lax.rem(i, N_COL)]
                ).wait_send()
            )

    sends.append(sent_sum)
    gather_h = []
    for h in range(2):

        def take_piece(k, h=h):
            @pl.when(lax.div(lax.rem(z + NZ - k, NZ), HALF_COL) == h)
            def _():
                gather_hz.arrival(k, lambda i: hz_all.at[lax.rem(i, N_COL)]).wait_recv()

        gather_hz.each(take_piece)
        part = pl.ds(h * HALF_COL, HALF_COL)
        h_all[pl.ds(y, 1), part] = hz_all[part][None]
        gather_h.append(y_axis(6 + h))
        sends.append(
            gather_h[h].start(
                lambda i, part=part: hz_all.at[part], lambda i, part=part: h_all.at[i, part]
            )
        )
    for h in range(2):
        gather_h[h].wait_recv(lambda i: h_all.at[i, pl.ds(h * HALF_COL, HALF_COL)])
        for r in range(NY):
            for c in range(h * HALF_COL, (h + 1) * HALF_COL):
                rows = slice(r * ROW_PIECE, (r + 1) * ROW_PIECE)
                head_ref[rows, c * 128 : (c + 1) * 128] = h_all[r, c].astype(F32)

    for wait in sends:
        wait()


def place(q_ref, p_ref, h_ref, q_out, p_out, h_out, sem):
    copies = [
        pltpu.make_async_copy(src, dst, sem.at[i])
        for i, (src, dst) in enumerate(((h_ref, h_out), (q_ref, q_out), (p_ref, p_out)))
    ]
    for copy in copies:
        copy.start()
    for copy in copies:
        copy.wait()


def shards(
    query_states, passage_states, head_weight, candidates, counts, teacher_scores, owner_map
):
    vmem = pltpu.VMEM
    scratch = [
        vmem((NY, ROWS, D), BF),
        vmem((NZ, 16, HALF), BF),
        vmem((NG, 16, HALF), BF),
        vmem((NY, ROWS, PB), F32),
        vmem((NY, 2, QB), F32),
        vmem((NZ, 16, HALF), BF),
        vmem((NY, ROWS, D), BF),
        vmem((NG, 16, HALF), BF),
        vmem((NY, 2, ROW_PIECE, HALF), BF),
        vmem((NZ, ROW_PIECE, 128), BF),
        vmem((N_COL, ROW_PIECE, 128), BF),
        vmem((NY, N_COL, ROW_PIECE, 128), BF),
        vmem((OWN, D), BF),
        vmem((1, 16, HALF), BF),
        vmem((D, D), BF),
        vmem((ROWS, CAND), jnp.int32),
        pltpu.SMEM((ROWS,), jnp.int32),
        vmem((ROWS, CAND), F32),
        vmem((1, POOL), jnp.int32),
        vmem((ROWS, CAND), jnp.int32),
        vmem((ROWS, CAND), jnp.int32),
        vmem((4, ROWS, CAND), F32),
        vmem((ROWS * NY, PB), F32),
        vmem((NY, ROWS, PB), F32),
        vmem((2, QB), F32),
        vmem((NZ, 16, HALF), BF),
        vmem((NY, ROWS, D), BF),
        vmem((NY, 2, ROW_PIECE, HALF), BF),
        vmem((N_COL, ROW_PIECE, 128), BF),
        vmem((NY, ROWS, D), BF),
        vmem((PB, D), BF),
        vmem((PB, D), BF),
        vmem((NG * OWN, D), BF),
        vmem((NG * OWN, D), F32),
        vmem((NG * OWN, D), F32),
        vmem((NG * OWN, D), F32),
        pltpu.SemaphoreType.DMA((7,)),
        pltpu.SemaphoreType.DMA((9, NY - 1)),
        pltpu.SemaphoreType.DMA((9, NY - 1)),
        pltpu.SemaphoreType.DMA((4, NZ - 1)),
        pltpu.SemaphoreType.DMA((4, NZ - 1)),
        pltpu.SemaphoreType.DMA((2, NG - 1)),
        pltpu.SemaphoreType.DMA((2, NG - 1)),
    ]
    outs = (((ROWS, D), BF), ((OWN, D), BF), ((OUT_ROWS, D), F32))
    results = pl.pallas_call(
        kernel,
        out_shape=tuple(vmem(shape, dtype) for shape, dtype in outs),
        in_specs=[pl.BlockSpec(memory_space=pl.ANY)] * 7,
        out_specs=tuple([pl.BlockSpec(memory_space=vmem)] * 3),
        scratch_shapes=scratch,
        name="distill",
        compiler_params=pltpu.CompilerParams(
            collective_id=0, has_side_effects=True, vmem_limit_bytes=61 * 1024 * 1024
        ),
    )(query_states, passage_states, head_weight, candidates, counts, teacher_scores, owner_map)
    return pl.pallas_call(
        place,
        out_shape=tuple(jax.ShapeDtypeStruct(shape, dtype) for shape, dtype in outs),
        in_specs=[pl.BlockSpec(memory_space=pl.ANY)] * 3,
        out_specs=tuple([pl.BlockSpec(memory_space=pl.ANY)] * 3),
        scratch_shapes=[pltpu.SemaphoreType.DMA((3,))],
        name="place",
    )(*(pltpu.with_memory_space_constraint(result, vmem) for result in results))


def solution(mesh):
    rows = P(("grp", "dev"), None)
    in_specs = (rows, rows, P(), rows, P(("grp", "dev")), rows, P("grp", None))
    out_specs = (rows, rows, P("grp", None))
    return jax.shard_map(shards, mesh=mesh, in_specs=in_specs, out_specs=out_specs, check_vma=False)
```

```python
import functools

import jax
import jax.numpy as jnp
from jax import lax
from jax.experimental import pallas as pl
from jax.experimental.pallas import tpu as pltpu
from jax.sharding import PartitionSpec as P

MESH = pl.DeviceIdType.MESH
NG, NZ, NY = 8, 12, 8
ROWS, OWN, D, CAND, POOL = 32, 8, 1024, 256, 768
QB = NY * ROWS
PB = 128
HALF = D // 2
OUT_ROWS = D // NG
ROW_PIECE = OUT_ROWS // NY
N_COL = D // 128
HALF_COL = N_COL // 2
BF, F32 = jnp.bfloat16, jnp.float32
FAR = -1.0e30
Q_ORDER = (0, 2, 6, 1, 7, 3, 5, 4)


def dot(a, b, ca, cb):
    return lax.dot_general(a, b, (((ca,), (cb,)), ((), ())), preferred_element_type=F32)


def fold(rows):
    return jnp.concatenate([rows[:, :, :HALF], rows[:, :, HALF:]], axis=1).astype(BF)


def unfold(block):
    wide = block.astype(F32)
    wide = jnp.concatenate([wide[:, :OWN, :], wide[:, OWN:, :]], axis=2)
    return wide.reshape(wide.shape[0] * OWN, D)


def far_first(n):
    return sorted(range(1, n), key=lambda k: -min(k, n - k))


class Exchange:
    def __init__(self, n, me, device, send_sem, recv_sem):
        self.n, self.me, self.device = n, me, device
        self.send_sem, self.recv_sem = send_sem, recv_sem

    def copy(self, k, src, dst):
        peer = lax.rem(self.me + k, self.n)
        return pltpu.make_async_remote_copy(
            src_ref=src(peer),
            dst_ref=dst(self.me),
            send_sem=self.send_sem.at[k - 1],
            recv_sem=self.recv_sem.at[k - 1],
            device_id=self.device(peer),
            device_id_type=MESH,
        )

    def arrival(self, k, dst):
        sender = lax.rem(self.me + self.n - k, self.n)
        return pltpu.make_async_remote_copy(
            src_ref=dst(sender),
            dst_ref=dst(sender),
            send_sem=self.send_sem.at[k - 1],
            recv_sem=self.recv_sem.at[k - 1],
            device_id=self.device(sender),
            device_id_type=MESH,
        )

    def each(self, body):
        def step(k, carry):
            body(k)
            return carry

        lax.fori_loop(1, self.n, step, 0)

    def far_first(self, body):
        for k in far_first(self.n):
            body(k)

    def start(self, src, dst):
        self.far_first(lambda k: self.copy(k, src, dst).start())
        return lambda: self.each(lambda k: self.copy(k, src, dst).wait_send())

    def wait_recv(self, dst):
        self.each(lambda k: self.arrival(k, dst).wait_recv())


def kernel(
    qs_hbm, ps_hbm, w_hbm, cand_hbm, counts_hbm, teach_hbm, own_hbm,
    qgrad_ref, pgrad_ref, head_ref,
    qs_all, ps_all, pg_all, t_all, st_all, v_in, u_in, vg_all, h_in, hz_in, hz_all, h_all,
    ps_loc, ps_mine, w_ref, cand_ref, counts_ref, teach_ref, own_ref,
    b_ref, y_ref, parts_ref, tb_ref, t_out, st_out, v_out, u_out, h_out, hz_out,
    q_ref, p128_ref, ps128_ref, p64_ref, ps64_ref, v64_ref, vw_ref,
    local_sem, ysend, yrecv, zsend, zrecv, gsend, grecv,
):
    g = lax.axis_index("grp")
    d = lax.axis_index("dev")
    z, y = d // NY, lax.rem(d, NY)
    scale = D ** -0.5

    def on_y(i):
        return (g, z * NY + i)

    def on_z(i):
        return (g, i * NY + y)

    def on_g(i):
        return (i, d)

    def y_axis(s):
        return Exchange(NY, y, on_y, ysend.at[s], yrecv.at[s])

    def z_axis(s):
        return Exchange(NZ, z, on_z, zsend.at[s], zrecv.at[s])

    def g_axis(s):
        return Exchange(NG, g, on_g, gsend.at[s], grecv.at[s])

    sends = []

    barrier = pltpu.get_barrier_semaphore()
    for n, me, device in ((NZ, z, on_z), (NY, y, on_y), (NG, g, on_g)):
        for k in far_first(n):
            pl.semaphore_signal(
                barrier, inc=1, device_id=device(lax.rem(me + k, n)), device_id_type=MESH
            )

    locals_ = [
        pltpu.make_async_copy(src, dst, local_sem.at[i])
        for i, (src, dst) in enumerate(
            [
                (ps_hbm, ps_loc),
                (qs_hbm, qs_all.at[y]),
                (cand_hbm, cand_ref),
                (own_hbm, own_ref),
                (counts_hbm, counts_ref),
                (teach_hbm, teach_ref),
                (w_hbm, w_ref),
            ]
        )
    ]
    for copy in locals_:
        copy.start()
    locals_[0].wait()
    mine = fold(ps_loc[...].astype(F32)[None])
    ps_mine[...] = mine
    ps_all[pl.ds(z, 1)] = mine
    pg_all[pl.ds(g, 1)] = mine
    locals_[1].wait()

    for copy in locals_[2:6]:
        copy.wait()
    row_id = lax.broadcasted_iota(jnp.int32, (ROWS, 128), 0)
    lane_id = lax.broadcasted_iota(jnp.int32, (ROWS, 128), 1)
    limit = jnp.zeros((ROWS, 128), jnp.int32)
    for i in range(ROWS):
        limit = jnp.where(row_id == i, counts_ref[i], limit)
    storage = []
    for c in range(CAND // 128):
        ids = cand_ref[:, c * 128 : (c + 1) * 128]
        low, high = ids & 127, ids >> 7
        row = jnp.zeros((ROWS, 128), jnp.int32)
        for t in range(POOL // 128):
            table = jnp.broadcast_to(own_ref[:, t * 128 : (t + 1) * 128], (ROWS, 128))
            picked = jnp.take_along_axis(table, low, axis=1, mode="promise_in_bounds")
            row = jnp.where(high == t, picked, row)
        storage.append(row)
    storage = jnp.concatenate(storage, axis=1)
    b_ref[...] = ((storage >> 6) << 3) | (storage & 7)
    y_ref[...] = (storage >> 3) & 7
    slot_id = jnp.concatenate([lane_id, lane_id + 128], axis=1)
    valid = slot_id < jnp.concatenate([limit, limit], axis=1)
    values = teach_ref[...]
    top = jnp.max(jnp.where(valid, values, -jnp.inf), axis=1, keepdims=True)
    weights = jnp.where(valid, jnp.exp(jnp.where(valid, values - top, 0.0)), 0.0)
    teacher = weights / jnp.sum(weights, axis=1, keepdims=True)
    part = teacher.astype(BF).astype(F32)
    parts_ref[0] = part
    rest = teacher - part
    part = rest.astype(BF).astype(F32)
    parts_ref[1] = part
    parts_ref[2] = rest - part
    parts_ref[3] = jnp.where(valid, 1.0, 0.0)

    pl.semaphore_wait(barrier, NZ + NY + NG - 3)
    gather_q, gather_p, gather_pg = y_axis(0), z_axis(0), g_axis(0)

    def send_block(k):
        copy = gather_q.copy(k, lambda i: qs_all.at[y], lambda i: qs_all.at[i])
        copy.start()
        sends.append(copy.wait_send)

    send_block(2)
    send_block(6)
    sends.append(gather_p.start(lambda i: ps_mine.at[0], lambda i: ps_all.at[i]))
    sends.append(gather_pg.start(lambda i: ps_mine.at[0], lambda i: pg_all.at[i]))
    block_id = lax.broadcasted_iota(jnp.int32, (PB, CAND), 0)
    owner_id = lax.broadcasted_iota(jnp.int32, (NY, CAND), 0)

    def densify(i, carry):
        hot = jnp.where(block_id == b_ref[pl.ds(i, 1), :], 1.0, 0.0).astype(BF)
        mask = owner_id == y_ref[pl.ds(i, 1), :]
        lhs = jnp.concatenate(
            [jnp.where(mask, parts_ref[n, pl.ds(i, 1), :], 0.0) for n in range(4)], axis=0
        ).astype(BF)
        out = dot(lhs, hot, 1, 1)
        dense = out[0:8] + (out[8:16] + out[16:24])
        tb_ref[pl.ds(pl.multiple_of(i * NY, NY), NY), :] = jnp.where(out[24:32] > 0.5, dense, -1.0)
        return carry

    lax.fori_loop(0, ROWS // 2, densify, 0, unroll=4)
    send_block(1)
    send_block(7)
    lax.fori_loop(ROWS // 2, ROWS, densify, 0, unroll=4)
    for k, shift, s, n in ((2, 2, 0, 3), (2, 1, 0, 2), (6, -2, 8, 0), (6, -1, 0, 4)):
        if abs(shift) == 2:
            gather_q.arrival(k, lambda i: qs_all.at[i]).wait_recv()
        block = qs_all.at[lax.rem(y + NY - k, NY)]
        if abs(shift) == 2:
            block = block.at[pl.ds(ROWS // 2 * (shift < 0), ROWS // 2)]
        copy = pltpu.make_async_remote_copy(
            src_ref=block,
            dst_ref=block,
            send_sem=ysend.at[s, n],
            recv_sem=yrecv.at[s, n],
            device_id=on_y(lax.rem(y + shift + NY, NY)),
            device_id_type=MESH,
        )
        copy.start()
        sends.append(copy.wait_send)

    for i in range(NY):
        t_out[i] = tb_ref[pl.ds(i, ROWS, stride=NY), :]
    t_all[pl.ds(y, 1)] = t_out[pl.ds(y, 1)]
    gather_t = y_axis(1)
    sends.append(gather_t.start(lambda i: t_out.at[i], lambda i: t_all.at[i]))


    locals_[6].wait()
    gather_p.wait_recv(lambda i: ps_all.at[i])
    ps128_ref[...] = jnp.concatenate(
        [unfold(ps_all[...]), jnp.zeros((PB - NZ * OWN, D), F32)], axis=0
    ).astype(BF)
    p128_ref[...] = dot(ps128_ref[...], w_ref[...], 1, 0).astype(BF)
    for part in (Q_ORDER[:5], Q_ORDER[5:]):
        spots = []
        for k in part:
            if k in (1, 7, 3, 5):
                gather_q.arrival(k, lambda i: qs_all.at[i]).wait_recv()
            spots.append(lax.rem(y + NY - k, NY))
            if k == 4:
                for s, n, start in ((0, 3, 0), (8, 0, ROWS // 2)):
                    block = qs_all.at[spots[-1], pl.ds(start, ROWS // 2)]
                    pltpu.make_async_copy(block, block, yrecv.at[s, n]).wait()
        some = jnp.concatenate([qs_all[pl.ds(i, 1)] for i in spots], axis=0)
        done = dot(some.reshape(len(spots) * ROWS, D), w_ref[...], 1, 0).astype(BF)
        for n, i in enumerate(spots):
            q_ref[pl.ds(i, 1)] = done[n * ROWS : (n + 1) * ROWS][None]
    qs_block = qs_all[...].reshape(QB, D)


    score = scale * dot(p128_ref[...], q_ref[...].reshape(QB, D), 1, 1)
    gather_t.wait_recv(lambda i: t_all.at[i])
    teach = t_all[...].reshape(QB, PB).T
    used = teach >= 0.0
    local_top = jnp.max(jnp.where(used, score, FAR), axis=0, keepdims=True)
    expo = jnp.where(used, jnp.exp(jnp.where(used, score - local_top, 0.0)), 0.0)
    local_sum = jnp.sum(expo, axis=0, keepdims=True)
    stats = jnp.where(
        lax.broadcasted_iota(jnp.int32, (2, QB), 0) == 0, local_top, local_sum
    )
    st_out[...] = stats
    st_all[pl.ds(y, 1)] = stats[None]
    stats_x = y_axis(2)
    sends.append(stats_x.start(lambda i: st_out, lambda i: st_all.at[i]))
    gather_pg.wait_recv(lambda i: pg_all.at[i])
    ps64_ref[...] = unfold(pg_all[...])
    p64_ref[...] = dot(ps64_ref[...].astype(BF), w_ref[...], 1, 0).astype(BF)
    stats_x.wait_recv(lambda i: st_all.at[i])
    tops = st_all[:, 0:1, :]
    top = jnp.max(tops, axis=0)
    total = jnp.sum(st_all[:, 1:2, :] * jnp.exp(tops - top[None]), axis=0)
    student = expo * (jnp.exp(local_top - top) / total)
    dscore = jnp.where(used, 256.0 * (student - teach), 0.0).astype(BF)


    v_part = scale * dot(dscore, qs_block, 1, 0)
    v_out[...] = fold(v_part[: NZ * OWN].reshape(NZ, OWN, D))
    v_in[pl.ds(z, 1)] = v_out[pl.ds(z, 1)]
    reduce_v = z_axis(1)
    sends.append(reduce_v.start(lambda i: v_out.at[i], lambda i: v_in.at[i]))
    u_part = scale * dot(dscore.astype(F32).T.astype(BF), ps128_ref[...], 1, 0)
    u_out[...] = u_part.astype(BF).reshape(NY, ROWS, D)
    u_in[pl.ds(y, 1)] = u_out[pl.ds(y, 1)]
    reduce_u = y_axis(3)
    sends.append(reduce_u.start(lambda i: u_out.at[i], lambda i: u_in.at[i]))


    reduce_v.wait_recv(lambda i: v_in.at[i])
    v_sum = jnp.sum(v_in[...].astype(F32), axis=0)
    vg_all[pl.ds(g, 1)] = v_sum.astype(BF)[None]
    gather_v = g_axis(1)
    sends.append(gather_v.start(lambda i: vg_all.at[g], lambda i: vg_all.at[i]))
    gather_v.wait_recv(lambda i: vg_all.at[i])
    v64_ref[...] = unfold(vg_all[...])
    cols = pl.ds(pl.multiple_of(g * OUT_ROWS, OUT_ROWS), OUT_ROWS)
    left = jnp.concatenate([v64_ref[:, cols], ps64_ref[:, cols]], axis=0).T.astype(BF)
    v64 = v64_ref[...].astype(BF)
    reduce_h = []
    for h in range(2):
        half = slice(h * HALF, (h + 1) * HALF)
        vw = dot(v64, w_ref[:, half], 1, 0).astype(BF)
        vw_ref[:, half] = vw.astype(F32)
        right = jnp.concatenate([p64_ref[:, half], vw], axis=0)
        h_out[:, h] = dot(left, right, 1, 0).astype(BF).reshape(NY, ROW_PIECE, HALF)
        h_in[pl.ds(y, 1), h] = h_out[pl.ds(y, 1), h]
        reduce_h.append(y_axis(4 + h))
        sends.append(
            reduce_h[h].start(lambda i, h=h: h_out.at[i, h], lambda i, h=h: h_in.at[i, h])
        )

    reduce_u.wait_recv(lambda i: u_in.at[i])
    u_sum = jnp.sum(u_in[...].astype(F32), axis=0).astype(BF)
    gq = dot(u_sum, w_ref[...], 1, 0)
    gp = vw_ref[pl.ds(pl.multiple_of(g * OWN, OWN), OWN), :]
    rows = jnp.concatenate([gq, gp, gp], axis=0).astype(BF)
    grads = dot(rows, w_ref[...], 1, 1)
    qgrad_ref[...] = grads[:ROWS].astype(BF)
    pgrad_ref[...] = grads[ROWS : ROWS + OWN].astype(BF)


    reduce_hz, gather_hz = z_axis(2), z_axis(3)
    for h in range(2):
        reduce_h[h].wait_recv(lambda i: h_in.at[i, h])
        h_sum = jnp.sum(h_in[:, h].astype(F32), axis=0).astype(BF)
        for i in range(HALF_COL):
            hz_out[h * HALF_COL + i] = h_sum[:, i * 128 : (i + 1) * 128]

        def owner(k, h=h):
            return lax.div(lax.rem(z + k, NZ), HALF_COL) == h

        def piece(k):
            return reduce_hz.copy(
                k, lambda i: hz_out.at[lax.rem(i, N_COL)], lambda i: hz_in.at[i]
            )

        def send_piece(k, owner=owner):
            @pl.when(owner(k))
            def _():
                piece(k).start()

        def sent_piece(k, owner=owner):
            @pl.when(owner(k))
            def _():
                piece(k).wait_send()

        reduce_hz.far_first(send_piece)
        sends.append(lambda sent_piece=sent_piece: reduce_hz.each(sent_piece))

    @pl.when(z < N_COL)
    def _():
        spot = lax.rem(z, N_COL)
        hz_in[pl.ds(z, 1)] = hz_out[pl.ds(spot, 1)]
        reduce_hz.wait_recv(lambda i: hz_in.at[i])
        hz_all[pl.ds(spot, 1)] = jnp.sum(hz_in[...].astype(F32), axis=0).astype(BF)[None]
        gather_hz.start(lambda i: hz_all.at[spot], lambda i: hz_all.at[lax.rem(i, N_COL)])

    def sent_sum():
        @pl.when(z < N_COL)
        def _():
            gather_hz.each(
                lambda k: gather_hz.copy(
                    k, lambda i: hz_all.at[0], lambda i: hz_all.at[lax.rem(i, N_COL)]
                ).wait_send()
            )

    sends.append(sent_sum)
    gather_h = []
    for h in range(2):

        def take_piece(k, h=h):
            @pl.when(lax.div(lax.rem(z + NZ - k, NZ), HALF_COL) == h)
            def _():
                gather_hz.arrival(k, lambda i: hz_all.at[lax.rem(i, N_COL)]).wait_recv()

        gather_hz.each(take_piece)
        part = pl.ds(h * HALF_COL, HALF_COL)
        h_all[pl.ds(y, 1), part] = hz_all[part][None]
        gather_h.append(y_axis(6 + h))
        sends.append(
            gather_h[h].start(
                lambda i, part=part: hz_all.at[part], lambda i, part=part: h_all.at[i, part]
            )
        )
    for h in range(2):
        gather_h[h].wait_recv(lambda i: h_all.at[i, pl.ds(h * HALF_COL, HALF_COL)])
        for r in range(NY):
            for c in range(h * HALF_COL, (h + 1) * HALF_COL):
                rows = slice(r * ROW_PIECE, (r + 1) * ROW_PIECE)
                head_ref[rows, c * 128 : (c + 1) * 128] = h_all[r, c].astype(F32)

    for wait in sends:
        wait()


def place(q_ref, p_ref, h_ref, q_out, p_out, h_out, sem):
    copies = [
        pltpu.make_async_copy(src, dst, sem.at[i])
        for i, (src, dst) in enumerate(((h_ref, h_out), (q_ref, q_out), (p_ref, p_out)))
    ]
    for copy in copies:
        copy.start()
    for copy in copies:
        copy.wait()


def shards(
    query_states, passage_states, head_weight, candidates, counts, teacher_scores, owner_map
):
    vmem = pltpu.VMEM
    scratch = [
        vmem((NY, ROWS, D), BF),
        vmem((NZ, 16, HALF), BF),
        vmem((NG, 16, HALF), BF),
        vmem((NY, ROWS, PB), F32),
        vmem((NY, 2, QB), F32),
        vmem((NZ, 16, HALF), BF),
        vmem((NY, ROWS, D), BF),
        vmem((NG, 16, HALF), BF),
        vmem((NY, 2, ROW_PIECE, HALF), BF),
        vmem((NZ, ROW_PIECE, 128), BF),
        vmem((N_COL, ROW_PIECE, 128), BF),
        vmem((NY, N_COL, ROW_PIECE, 128), BF),
        vmem((OWN, D), BF),
        vmem((1, 16, HALF), BF),
        vmem((D, D), BF),
        vmem((ROWS, CAND), jnp.int32),
        pltpu.SMEM((ROWS,), jnp.int32),
        vmem((ROWS, CAND), F32),
        vmem((1, POOL), jnp.int32),
        vmem((ROWS, CAND), jnp.int32),
        vmem((ROWS, CAND), jnp.int32),
        vmem((4, ROWS, CAND), F32),
        vmem((ROWS * NY, PB), F32),
        vmem((NY, ROWS, PB), F32),
        vmem((2, QB), F32),
        vmem((NZ, 16, HALF), BF),
        vmem((NY, ROWS, D), BF),
        vmem((NY, 2, ROW_PIECE, HALF), BF),
        vmem((N_COL, ROW_PIECE, 128), BF),
        vmem((NY, ROWS, D), BF),
        vmem((PB, D), BF),
        vmem((PB, D), BF),
        vmem((NG * OWN, D), BF),
        vmem((NG * OWN, D), F32),
        vmem((NG * OWN, D), F32),
        vmem((NG * OWN, D), F32),
        pltpu.SemaphoreType.DMA((7,)),
        pltpu.SemaphoreType.DMA((9, NY - 1)),
        pltpu.SemaphoreType.DMA((9, NY - 1)),
        pltpu.SemaphoreType.DMA((4, NZ - 1)),
        pltpu.SemaphoreType.DMA((4, NZ - 1)),
        pltpu.SemaphoreType.DMA((2, NG - 1)),
        pltpu.SemaphoreType.DMA((2, NG - 1)),
    ]
    outs = (((ROWS, D), BF), ((OWN, D), BF), ((OUT_ROWS, D), F32))
    results = pl.pallas_call(
        kernel,
        out_shape=tuple(vmem(shape, dtype) for shape, dtype in outs),
        in_specs=[pl.BlockSpec(memory_space=pl.ANY)] * 7,
        out_specs=tuple([pl.BlockSpec(memory_space=vmem)] * 3),
        scratch_shapes=scratch,
        name="distill",
        compiler_params=pltpu.CompilerParams(
            collective_id=0, has_side_effects=True, vmem_limit_bytes=61 * 1024 * 1024
        ),
    )(query_states, passage_states, head_weight, candidates, counts, teacher_scores, owner_map)
    return pl.pallas_call(
        place,
        out_shape=tuple(jax.ShapeDtypeStruct(shape, dtype) for shape, dtype in outs),
        in_specs=[pl.BlockSpec(memory_space=pl.ANY)] * 3,
        out_specs=tuple([pl.BlockSpec(memory_space=pl.ANY)] * 3),
        scratch_shapes=[pltpu.SemaphoreType.DMA((3,))],
        name="place",
    )(*(pltpu.with_memory_space_constraint(result, vmem) for result in results))


def solution(mesh):
    rows = P(("grp", "dev"), None)
    in_specs = (rows, rows, P(), rows, P(("grp", "dev")), rows, P("grp", None))
    out_specs = (rows, rows, P("grp", None))
    return jax.shard_map(shards, mesh=mesh, in_specs=in_specs, out_specs=out_specs, check_vma=False)
```

```python
import functools

import jax
import jax.numpy as jnp
from jax import lax
from jax.experimental import pallas as pl
from jax.experimental.pallas import tpu as pltpu
from jax.sharding import PartitionSpec as P

MESH = pl.DeviceIdType.MESH
NG, NZ, NY = 8, 12, 8
ROWS, OWN, D, CAND, POOL = 32, 8, 1024, 256, 768
QB = NY * ROWS
PB = 128
HALF = D // 2
OUT_ROWS = D // NG
ROW_PIECE = OUT_ROWS // NY
N_COL = D // 128
HALF_COL = N_COL // 2
BF, F32 = jnp.bfloat16, jnp.float32
FAR = -1.0e30
Q_ORDER = (0, 2, 6, 1, 7, 3, 5, 4)


def dot(a, b, ca, cb):
    return lax.dot_general(a, b, (((ca,), (cb,)), ((), ())), preferred_element_type=F32)


def fold(rows):
    return jnp.concatenate([rows[:, :, :HALF], rows[:, :, HALF:]], axis=1).astype(BF)


def unfold(block):
    wide = block.astype(F32)
    wide = jnp.concatenate([wide[:, :OWN, :], wide[:, OWN:, :]], axis=2)
    return wide.reshape(wide.shape[0] * OWN, D)


def far_first(n):
    return sorted(range(1, n), key=lambda k: -min(k, n - k))


class Exchange:
    def __init__(self, n, me, device, send_sem, recv_sem):
        self.n, self.me, self.device = n, me, device
        self.send_sem, self.recv_sem = send_sem, recv_sem

    def copy(self, k, src, dst):
        peer = lax.rem(self.me + k, self.n)
        return pltpu.make_async_remote_copy(
            src_ref=src(peer),
            dst_ref=dst(self.me),
            send_sem=self.send_sem.at[k - 1],
            recv_sem=self.recv_sem.at[k - 1],
            device_id=self.device(peer),
            device_id_type=MESH,
        )

    def arrival(self, k, dst):
        sender = lax.rem(self.me + self.n - k, self.n)
        return pltpu.make_async_remote_copy(
            src_ref=dst(sender),
            dst_ref=dst(sender),
            send_sem=self.send_sem.at[k - 1],
            recv_sem=self.recv_sem.at[k - 1],
            device_id=self.device(sender),
            device_id_type=MESH,
        )

    def each(self, body):
        def step(k, carry):
            body(k)
            return carry

        lax.fori_loop(1, self.n, step, 0)

    def far_first(self, body):
        for k in far_first(self.n):
            body(k)

    def start(self, src, dst):
        self.far_first(lambda k: self.copy(k, src, dst).start())
        return lambda: self.each(lambda k: self.copy(k, src, dst).wait_send())

    def wait_recv(self, dst):
        self.each(lambda k: self.arrival(k, dst).wait_recv())


def kernel(
    qs_hbm, ps_hbm, w_hbm, cand_hbm, counts_hbm, teach_hbm, own_hbm,
    qgrad_ref, pgrad_ref, head_ref,
    qs_all, ps_all, pg_all, t_all, st_all, v_in, u_in, vg_all, h_in, hz_in, hz_all, h_all,
    ps_loc, ps_mine, w_ref, cand_ref, counts_ref, teach_ref, own_ref,
    b_ref, y_ref, parts_ref, tb_ref, t_out, st_out, v_out, u_out, h_out, hz_out,
    q_ref, p128_ref, ps128_ref, p64_ref, ps64_ref, v64_ref, vw_ref,
    local_sem, ysend, yrecv, zsend, zrecv, gsend, grecv,
):
    g = lax.axis_index("grp")
    d = lax.axis_index("dev")
    z, y = d // NY, lax.rem(d, NY)
    scale = D ** -0.5

    def on_y(i):
        return (g, z * NY + i)

    def on_z(i):
        return (g, i * NY + y)

    def on_g(i):
        return (i, d)

    def y_axis(s):
        return Exchange(NY, y, on_y, ysend.at[s], yrecv.at[s])

    def z_axis(s):
        return Exchange(NZ, z, on_z, zsend.at[s], zrecv.at[s])

    def g_axis(s):
        return Exchange(NG, g, on_g, gsend.at[s], grecv.at[s])

    sends = []

    barrier = pltpu.get_barrier_semaphore()
    for n, me, device in ((NZ, z, on_z), (NY, y, on_y), (NG, g, on_g)):
        for k in far_first(n):
            pl.semaphore_signal(
                barrier, inc=1, device_id=device(lax.rem(me + k, n)), device_id_type=MESH
            )

    locals_ = [
        pltpu.make_async_copy(src, dst, local_sem.at[i])
        for i, (src, dst) in enumerate(
            [
                (ps_hbm, ps_loc),
                (qs_hbm, qs_all.at[y]),
                (cand_hbm, cand_ref),
                (own_hbm, own_ref),
                (counts_hbm, counts_ref),
                (teach_hbm, teach_ref),
                (w_hbm, w_ref),
            ]
        )
    ]
    for copy in locals_:
        copy.start()
    locals_[0].wait()
    mine = fold(ps_loc[...].astype(F32)[None])
    ps_mine[...] = mine
    ps_all[pl.ds(z, 1)] = mine
    pg_all[pl.ds(g, 1)] = mine
    locals_[1].wait()

    for copy in locals_[2:6]:
        copy.wait()
    row_id = lax.broadcasted_iota(jnp.int32, (ROWS, 128), 0)
    lane_id = lax.broadcasted_iota(jnp.int32, (ROWS, 128), 1)
    limit = jnp.zeros((ROWS, 128), jnp.int32)
    for i in range(ROWS):
        limit = jnp.where(row_id == i, counts_ref[i], limit)
    storage = []
    for c in range(CAND // 128):
        ids = cand_ref[:, c * 128 : (c + 1) * 128]
        low, high = ids & 127, ids >> 7
        row = jnp.zeros((ROWS, 128), jnp.int32)
        for t in range(POOL // 128):
            table = jnp.broadcast_to(own_ref[:, t * 128 : (t + 1) * 128], (ROWS, 128))
            picked = jnp.take_along_axis(table, low, axis=1, mode="promise_in_bounds")
            row = jnp.where(high == t, picked, row)
        storage.append(row)
    storage = jnp.concatenate(storage, axis=1)
    b_ref[...] = ((storage >> 6) << 3) | (storage & 7)
    y_ref[...] = (storage >> 3) & 7
    slot_id = jnp.concatenate([lane_id, lane_id + 128], axis=1)
    valid = slot_id < jnp.concatenate([limit, limit], axis=1)
    values = teach_ref[...]
    top = jnp.max(jnp.where(valid, values, -jnp.inf), axis=1, keepdims=True)
    weights = jnp.where(valid, jnp.exp(jnp.where(valid, values - top, 0.0)), 0.0)
    teacher = weights / jnp.sum(weights, axis=1, keepdims=True)
    part = teacher.astype(BF).astype(F32)
    parts_ref[0] = part
    rest = teacher - part
    part = rest.astype(BF).astype(F32)
    parts_ref[1] = part
    parts_ref[2] = rest - part
    parts_ref[3] = jnp.where(valid, 1.0, 0.0)

    pl.semaphore_wait(barrier, NZ + NY + NG - 3)
    gather_q, gather_p, gather_pg = y_axis(0), z_axis(0), g_axis(0)
    for k in (2, 6, 1, 7):
        copy = gather_q.copy(k, lambda i: qs_all.at[y], lambda i: qs_all.at[i])
        copy.start()
        sends.append(copy.wait_send)
    sends.append(gather_p.start(lambda i: ps_mine.at[0], lambda i: ps_all.at[i]))
    sends.append(gather_pg.start(lambda i: ps_mine.at[0], lambda i: pg_all.at[i]))
    block_id = lax.broadcasted_iota(jnp.int32, (PB, CAND), 0)
    owner_id = lax.broadcasted_iota(jnp.int32, (NY, CAND), 0)

    def densify(i, carry):
        hot = jnp.where(block_id == b_ref[pl.ds(i, 1), :], 1.0, 0.0).astype(BF)
        mask = owner_id == y_ref[pl.ds(i, 1), :]
        lhs = jnp.concatenate(
            [jnp.where(mask, parts_ref[n, pl.ds(i, 1), :], 0.0) for n in range(4)], axis=0
        ).astype(BF)
        out = dot(lhs, hot, 1, 1)
        dense = out[0:8] + (out[8:16] + out[16:24])
        tb_ref[pl.ds(pl.multiple_of(i * NY, NY), NY), :] = jnp.where(out[24:32] > 0.5, dense, -1.0)
        return carry

    lax.fori_loop(0, ROWS * 3 // 4, densify, 0, unroll=4)

    for k, shift, s, n in ((2, 1, 0, 2), (6, -1, 0, 4), (2, 2, 0, 3), (6, -2, 8, 0)):
        if abs(shift) == 1:
            gather_q.arrival(k, lambda i: qs_all.at[i]).wait_recv()
        block = qs_all.at[lax.rem(y + NY - k, NY)]
        if abs(shift) == 2:
            block = block.at[pl.ds(ROWS // 2 * (shift < 0), ROWS // 2)]
        copy = pltpu.make_async_remote_copy(
            src_ref=block,
            dst_ref=block,
            send_sem=ysend.at[s, n],
            recv_sem=yrecv.at[s, n],
            device_id=on_y(lax.rem(y + shift + NY, NY)),
            device_id_type=MESH,
        )
        copy.start()
        sends.append(copy.wait_send)

    lax.fori_loop(ROWS * 3 // 4, ROWS, densify, 0, unroll=4)
    for i in range(NY):
        t_out[i] = tb_ref[pl.ds(i, ROWS, stride=NY), :]
    t_all[pl.ds(y, 1)] = t_out[pl.ds(y, 1)]
    gather_t = y_axis(1)
    sends.append(gather_t.start(lambda i: t_out.at[i], lambda i: t_all.at[i]))


    locals_[6].wait()
    gather_p.wait_recv(lambda i: ps_all.at[i])
    ps128_ref[...] = jnp.concatenate(
        [unfold(ps_all[...]), jnp.zeros((PB - NZ * OWN, D), F32)], axis=0
    ).astype(BF)
    p128_ref[...] = dot(ps128_ref[...], w_ref[...], 1, 0).astype(BF)
    for part in (Q_ORDER[:5], Q_ORDER[5:]):
        spots = []
        for k in part:
            if k in (1, 7, 3, 5):
                gather_q.arrival(k, lambda i: qs_all.at[i]).wait_recv()
            spots.append(lax.rem(y + NY - k, NY))
            if k == 4:
                for s, n, start in ((0, 3, 0), (8, 0, ROWS // 2)):
                    block = qs_all.at[spots[-1], pl.ds(start, ROWS // 2)]
                    pltpu.make_async_copy(block, block, yrecv.at[s, n]).wait()
        some = jnp.concatenate([qs_all[pl.ds(i, 1)] for i in spots], axis=0)
        done = dot(some.reshape(len(spots) * ROWS, D), w_ref[...], 1, 0).astype(BF)
        for n, i in enumerate(spots):
            q_ref[pl.ds(i, 1)] = done[n * ROWS : (n + 1) * ROWS][None]
    qs_block = qs_all[...].reshape(QB, D)


    score = scale * dot(p128_ref[...], q_ref[...].reshape(QB, D), 1, 1)
    gather_t.wait_recv(lambda i: t_all.at[i])
    teach = t_all[...].reshape(QB, PB).T
    used = teach >= 0.0
    local_top = jnp.max(jnp.where(used, score, FAR), axis=0, keepdims=True)
    expo = jnp.where(used, jnp.exp(jnp.where(used, score - local_top, 0.0)), 0.0)
    local_sum = jnp.sum(expo, axis=0, keepdims=True)
    stats = jnp.where(
        lax.broadcasted_iota(jnp.int32, (2, QB), 0) == 0, local_top, local_sum
    )
    st_out[...] = stats
    st_all[pl.ds(y, 1)] = stats[None]
    stats_x = y_axis(2)
    sends.append(stats_x.start(lambda i: st_out, lambda i: st_all.at[i]))
    gather_pg.wait_recv(lambda i: pg_all.at[i])
    ps64_ref[...] = unfold(pg_all[...])
    p64_ref[...] = dot(ps64_ref[...].astype(BF), w_ref[...], 1, 0).astype(BF)
    stats_x.wait_recv(lambda i: st_all.at[i])
    tops = st_all[:, 0:1, :]
    top = jnp.max(tops, axis=0)
    total = jnp.sum(st_all[:, 1:2, :] * jnp.exp(tops - top[None]), axis=0)
    student = expo * (jnp.exp(local_top - top) / total)
    dscore = jnp.where(used, 256.0 * (student - teach), 0.0).astype(BF)


    v_part = scale * dot(dscore, qs_block, 1, 0)
    v_out[...] = fold(v_part[: NZ * OWN].reshape(NZ, OWN, D))
    v_in[pl.ds(z, 1)] = v_out[pl.ds(z, 1)]
    reduce_v = z_axis(1)
    sends.append(reduce_v.start(lambda i: v_out.at[i], lambda i: v_in.at[i]))
    u_part = scale * dot(dscore.astype(F32).T.astype(BF), ps128_ref[...], 1, 0)
    u_out[...] = u_part.astype(BF).reshape(NY, ROWS, D)
    u_in[pl.ds(y, 1)] = u_out[pl.ds(y, 1)]
    reduce_u = y_axis(3)
    sends.append(reduce_u.start(lambda i: u_out.at[i], lambda i: u_in.at[i]))


    reduce_v.wait_recv(lambda i: v_in.at[i])
    v_sum = jnp.sum(v_in[...].astype(F32), axis=0)
    vg_all[pl.ds(g, 1)] = v_sum.astype(BF)[None]
    gather_v = g_axis(1)
    sends.append(gather_v.start(lambda i: vg_all.at[g], lambda i: vg_all.at[i]))
    gather_v.wait_recv(lambda i: vg_all.at[i])
    v64_ref[...] = unfold(vg_all[...])
    cols = pl.ds(pl.multiple_of(g * OUT_ROWS, OUT_ROWS), OUT_ROWS)
    left = jnp.concatenate([v64_ref[:, cols], ps64_ref[:, cols]], axis=0).T.astype(BF)
    v64 = v64_ref[...].astype(BF)
    reduce_h = []
    for h in range(2):
        half = slice(h * HALF, (h + 1) * HALF)
        vw = dot(v64, w_ref[:, half], 1, 0).astype(BF)
        vw_ref[:, half] = vw.astype(F32)
        right = jnp.concatenate([p64_ref[:, half], vw], axis=0)
        h_out[:, h] = dot(left, right, 1, 0).astype(BF).reshape(NY, ROW_PIECE, HALF)
        h_in[pl.ds(y, 1), h] = h_out[pl.ds(y, 1), h]
        reduce_h.append(y_axis(4 + h))
        sends.append(
            reduce_h[h].start(lambda i, h=h: h_out.at[i, h], lambda i, h=h: h_in.at[i, h])
        )

    reduce_u.wait_recv(lambda i: u_in.at[i])
    u_sum = jnp.sum(u_in[...].astype(F32), axis=0).astype(BF)
    gq = dot(u_sum, w_ref[...], 1, 0)
    gp = vw_ref[pl.ds(pl.multiple_of(g * OWN, OWN), OWN), :]
    rows = jnp.concatenate([gq, gp, gp], axis=0).astype(BF)
    grads = dot(rows, w_ref[...], 1, 1)
    qgrad_ref[...] = grads[:ROWS].astype(BF)
    pgrad_ref[...] = grads[ROWS : ROWS + OWN].astype(BF)


    reduce_hz, gather_hz = z_axis(2), z_axis(3)
    for h in range(2):
        reduce_h[h].wait_recv(lambda i: h_in.at[i, h])
        h_sum = jnp.sum(h_in[:, h].astype(F32), axis=0).astype(BF)
        for i in range(HALF_COL):
            hz_out[h * HALF_COL + i] = h_sum[:, i * 128 : (i + 1) * 128]

        def owner(k, h=h):
            return lax.div(lax.rem(z + k, NZ), HALF_COL) == h

        def piece(k):
            return reduce_hz.copy(
                k, lambda i: hz_out.at[lax.rem(i, N_COL)], lambda i: hz_in.at[i]
            )

        def send_piece(k, owner=owner):
            @pl.when(owner(k))
            def _():
                piece(k).start()

        def sent_piece(k, owner=owner):
            @pl.when(owner(k))
            def _():
                piece(k).wait_send()

        reduce_hz.far_first(send_piece)
        sends.append(lambda sent_piece=sent_piece: reduce_hz.each(sent_piece))

    @pl.when(z < N_COL)
    def _():
        spot = lax.rem(z, N_COL)
        hz_in[pl.ds(z, 1)] = hz_out[pl.ds(spot, 1)]
        reduce_hz.wait_recv(lambda i: hz_in.at[i])
        hz_all[pl.ds(spot, 1)] = jnp.sum(hz_in[...].astype(F32), axis=0).astype(BF)[None]
        gather_hz.start(lambda i: hz_all.at[spot], lambda i: hz_all.at[lax.rem(i, N_COL)])

    def sent_sum():
        @pl.when(z < N_COL)
        def _():
            gather_hz.each(
                lambda k: gather_hz.copy(
                    k, lambda i: hz_all.at[0], lambda i: hz_all.at[lax.rem(i, N_COL)]
                ).wait_send()
            )

    sends.append(sent_sum)
    gather_h = []
    for h in range(2):

        def take_piece(k, h=h):
            @pl.when(lax.div(lax.rem(z + NZ - k, NZ), HALF_COL) == h)
            def _():
                gather_hz.arrival(k, lambda i: hz_all.at[lax.rem(i, N_COL)]).wait_recv()

        gather_hz.each(take_piece)
        part = pl.ds(h * HALF_COL, HALF_COL)
        h_all[pl.ds(y, 1), part] = hz_all[part][None]
        gather_h.append(y_axis(6 + h))
        sends.append(
            gather_h[h].start(
                lambda i, part=part: hz_all.at[part], lambda i, part=part: h_all.at[i, part]
            )
        )
    for h in range(2):
        gather_h[h].wait_recv(lambda i: h_all.at[i, pl.ds(h * HALF_COL, HALF_COL)])
        for r in range(NY):
            for c in range(h * HALF_COL, (h + 1) * HALF_COL):
                rows = slice(r * ROW_PIECE, (r + 1) * ROW_PIECE)
                head_ref[rows, c * 128 : (c + 1) * 128] = h_all[r, c].astype(F32)

    for wait in sends:
        wait()


def place(q_ref, p_ref, h_ref, q_out, p_out, h_out, sem):
    copies = [
        pltpu.make_async_copy(src, dst, sem.at[i])
        for i, (src, dst) in enumerate(((h_ref, h_out), (q_ref, q_out), (p_ref, p_out)))
    ]
    for copy in copies:
        copy.start()
    for copy in copies:
        copy.wait()


def shards(
    query_states, passage_states, head_weight, candidates, counts, teacher_scores, owner_map
):
    vmem = pltpu.VMEM
    scratch = [
        vmem((NY, ROWS, D), BF),
        vmem((NZ, 16, HALF), BF),
        vmem((NG, 16, HALF), BF),
        vmem((NY, ROWS, PB), F32),
        vmem((NY, 2, QB), F32),
        vmem((NZ, 16, HALF), BF),
        vmem((NY, ROWS, D), BF),
        vmem((NG, 16, HALF), BF),
        vmem((NY, 2, ROW_PIECE, HALF), BF),
        vmem((NZ, ROW_PIECE, 128), BF),
        vmem((N_COL, ROW_PIECE, 128), BF),
        vmem((NY, N_COL, ROW_PIECE, 128), BF),
        vmem((OWN, D), BF),
        vmem((1, 16, HALF), BF),
        vmem((D, D), BF),
        vmem((ROWS, CAND), jnp.int32),
        pltpu.SMEM((ROWS,), jnp.int32),
        vmem((ROWS, CAND), F32),
        vmem((1, POOL), jnp.int32),
        vmem((ROWS, CAND), jnp.int32),
        vmem((ROWS, CAND), jnp.int32),
        vmem((4, ROWS, CAND), F32),
        vmem((ROWS * NY, PB), F32),
        vmem((NY, ROWS, PB), F32),
        vmem((2, QB), F32),
        vmem((NZ, 16, HALF), BF),
        vmem((NY, ROWS, D), BF),
        vmem((NY, 2, ROW_PIECE, HALF), BF),
        vmem((N_COL, ROW_PIECE, 128), BF),
        vmem((NY, ROWS, D), BF),
        vmem((PB, D), BF),
        vmem((PB, D), BF),
        vmem((NG * OWN, D), BF),
        vmem((NG * OWN, D), F32),
        vmem((NG * OWN, D), F32),
        vmem((NG * OWN, D), F32),
        pltpu.SemaphoreType.DMA((7,)),
        pltpu.SemaphoreType.DMA((9, NY - 1)),
        pltpu.SemaphoreType.DMA((9, NY - 1)),
        pltpu.SemaphoreType.DMA((4, NZ - 1)),
        pltpu.SemaphoreType.DMA((4, NZ - 1)),
        pltpu.SemaphoreType.DMA((2, NG - 1)),
        pltpu.SemaphoreType.DMA((2, NG - 1)),
    ]
    outs = (((ROWS, D), BF), ((OWN, D), BF), ((OUT_ROWS, D), F32))
    results = pl.pallas_call(
        kernel,
        out_shape=tuple(vmem(shape, dtype) for shape, dtype in outs),
        in_specs=[pl.BlockSpec(memory_space=pl.ANY)] * 7,
        out_specs=tuple([pl.BlockSpec(memory_space=vmem)] * 3),
        scratch_shapes=scratch,
        name="distill",
        compiler_params=pltpu.CompilerParams(
            collective_id=0, has_side_effects=True, vmem_limit_bytes=61 * 1024 * 1024
        ),
    )(query_states, passage_states, head_weight, candidates, counts, teacher_scores, owner_map)
    return pl.pallas_call(
        place,
        out_shape=tuple(jax.ShapeDtypeStruct(shape, dtype) for shape, dtype in outs),
        in_specs=[pl.BlockSpec(memory_space=pl.ANY)] * 3,
        out_specs=tuple([pl.BlockSpec(memory_space=pl.ANY)] * 3),
        scratch_shapes=[pltpu.SemaphoreType.DMA((3,))],
        name="place",
    )(*(pltpu.with_memory_space_constraint(result, vmem) for result in results))


def solution(mesh):
    rows = P(("grp", "dev"), None)
    in_specs = (rows, rows, P(), rows, P(("grp", "dev")), rows, P("grp", None))
    out_specs = (rows, rows, P("grp", None))
    return jax.shard_map(shards, mesh=mesh, in_specs=in_specs, out_specs=out_specs, check_vma=False)
```
